768 devices in a mesh: dom: 96 (over y, z), sub: 8 (over x, core).
Axes of the slice: x: 4, y: 8, z: 12, core: 2. Of those that a mesh axis runs over, the one named last changes fastest.
Arguments:
- diagonal: float32 [8, 96, 2, 320, 320], P('sub', 'dom'), may hold values from -1 to 2
- coupling: float32 [8, 96, 2, 3, 80, 80], P('sub', 'dom'), may hold values from -0.25 to 0.25
- start_block: float32 [8, 96, 2, 320, 128], P('sub', 'dom'), may hold values from -25 to 25
- shadow_block: float32 [8, 96, 2, 320, 128], P('sub', 'dom'), may hold values from -25 to 25
Outputs:
- last_basis: float32 [8, 96, 2, 320, 128], P('sub', 'dom')
- last_shadow: float32 [8, 96, 2, 320, 128], P('sub', 'dom')
- moments: float32 [5, 5, 128], replicated
The draws below stay inside these ranges and needn't reach their ends.
All inputs are finite; a program needn't handle non-finite values.
Results may differ from the reference program's by a relative error of at most 0.0003.
Values sent between devices are 32-bit elements; how exact they have to be, the bound alone decides.
A program may use at most 64 MiB of HBM per device.

```python
import math
import jax
import jax.numpy as jnp
from jax import lax

NVAR = 5
NQ = 4
P_SIZE = 320
F = 80
NV = 128
STEPS = 4
GX = 8
GY = 96
GZ = 2


def shared_field(key):
    normal_key, spread_key = jax.random.split(key)
    normals = jnp.clip(jax.random.normal(normal_key, (GX, GY, GZ, P_SIZE, NV), jnp.float32), -5.0, 5.0)
    spread = jax.random.uniform(spread_key, (GX, GY, GZ, 1, 1), jnp.float32)
    return (normals, spread)


def profile(steepness, spread):
    along_x = jnp.arange(GX, dtype=jnp.float32) / max(GX - 1, 1)
    along_y = jnp.arange(GY, dtype=jnp.float32) / max(GY - 1, 1)
    ramp_factor = (1.0 + steepness * along_x)[:, None, None, None, None] * (1.0 + steepness * along_y)[None, :, None, None, None]
    return 0.5 * jnp.sqrt(ramp_factor) * jnp.exp(0.6 * spread)


def draw_start_block(key, part):
    normals, spread = shared_field(key)
    result = normals * profile(2.0, spread)
    return result


def draw_shadow_block(key, part):
    normals, spread = shared_field(key)
    key = jax.random.fold_in(key, 12)
    others = jnp.clip(jax.random.normal(key, (GX, GY, GZ, P_SIZE, NV), jnp.float32), -5.0, 5.0)
    result = (0.6 * normals + 0.8 * others) * profile(2.0, spread)
    return result


def draw_diagonal(key, part):
    key = jax.random.fold_in(key, 13)
    noise_key, level_key = jax.random.split(key)
    noise_values = jnp.clip(jax.random.normal(noise_key, (GX, GY, GZ, P_SIZE, P_SIZE), jnp.float32), -5.0, 5.0)
    levels = jax.random.uniform(level_key, (GX, GY, GZ, P_SIZE, 1), jnp.float32)
    identity = (jnp.arange(P_SIZE)[:, None] == jnp.arange(P_SIZE)[None, :]).astype(jnp.float32)
    levels = 0.6 + 0.8 * levels
    return noise_values * (0.35 / math.sqrt(P_SIZE)) * (1.0 - identity) + levels * identity


def shard_levels(stream_key, dims, pieces, low, largest):
    def one(dim, shards_of):
        heights = jax.random.uniform(jax.random.fold_in(jax.random.fold_in(stream_key, 6), dim), (shards_of,), jnp.float32, low / len(pieces), largest / len(pieces))
        return jnp.repeat(jnp.exp(heights), dims[dim] // shards_of).reshape((-1,) + (1,) * (len(dims) - dim - 1))

    factor_of = one(*pieces[0])
    for cut in pieces[1:]:
        factor_of = factor_of * one(*cut)
    return factor_of


def bell_draw(own_key, shape, width, limit, cuts=(), kind=jnp.bfloat16):
    gain = shard_levels(own_key, shape, cuts, -0.22, 0.18) if cuts else 1.0
    values = jax.random.normal(own_key, shape, jnp.float32) * width * gain
    return jnp.minimum(jnp.maximum(values, -limit), limit).astype(kind)


def setup_inputs(seed: int = 0) -> dict:
    arg_keys = jax.random.split(jax.random.key(seed), 5)
    return {
        "diagonal": draw_diagonal(jax.random.fold_in(arg_keys[4], 71), 0),
        "coupling": bell_draw(arg_keys[1], (GX, GY, GZ, 3, F, F), (8 * F) ** -0.5, 0.25, ((0, 8), (1, 96)), jnp.float32),
        "start_block": draw_start_block(jax.random.fold_in(arg_keys[4], 71), 0),
        "shadow_block": draw_shadow_block(jax.random.fold_in(arg_keys[4], 71), 0),
    }


HIGH = lax.Precision.HIGHEST


def layers(source, begin_at, end_at, along_axis):
    return lax.slice_in_dim(source, begin_at, end_at, axis=along_axis)


def place_rows(added, values, node_axis, position):
    position_key = tuple([slice(None)] * node_axis + [position])
    return added.at[position_key].add(values)


def upper_terms(blocks, next_low):
    return jnp.einsum('xyzfg,sxyzgn->sxyzfn', blocks, next_low, precision=HIGH)


def lower_terms(blocks, high_face):
    return -jnp.einsum('xyzgf,sxyzgn->sxyzfn', blocks, high_face, precision=HIGH)


def face_terms(stacked, coupling):
    members, count_x, count_y, count_z, size_p, columns = stacked.shape
    node_grid = stacked.reshape(members, count_x, count_y, count_z, NVAR, NQ, NQ, NQ, columns)
    face_size = NVAR * NQ * NQ
    added = jnp.zeros_like(node_grid)
    for direction in range(3):
        node_axis = 5 + direction
        grid_axis = 1 + direction
        low_face = lax.index_in_dim(node_grid, 0, node_axis, keepdims=False)
        face_shape = low_face.shape
        low_face = low_face.reshape(members, count_x, count_y, count_z, face_size, columns)
        high_face = lax.index_in_dim(node_grid, NQ - 1, node_axis, keepdims=False).reshape(low_face.shape)
        blocks = coupling[:, :, :, direction]
        layer_count = low_face.shape[grid_axis]
        zero_layer = jnp.zeros_like(layers(low_face, 0, 1, grid_axis))
        next_low = jnp.concatenate([layers(low_face, 1, layer_count, grid_axis), zero_layer], axis=grid_axis)
        upper_rows = upper_terms(blocks, next_low)
        product = lower_terms(layers(blocks, 0, layer_count - 1, grid_axis - 1), layers(high_face, 0, layer_count - 1, grid_axis))
        lower_rows = jnp.concatenate([zero_layer, product], axis=grid_axis)
        added = place_rows(added, upper_rows.reshape(face_shape), node_axis, NQ - 1)
        added = place_rows(added, lower_rows.reshape(face_shape), node_axis, 0)
    return added.reshape(stacked.shape)


def apply_pair(stacked, diagonal, coupling):
    face_part = face_terms(stacked, coupling)
    forward = jnp.einsum('xyzpq,xyzqn->xyzpn', diagonal, stacked[0], precision=HIGH) + face_part[0]
    backward = jnp.einsum('xyzqp,xyzqn->xyzpn', diagonal, stacked[1], precision=HIGH) - face_part[1]
    return jnp.stack([forward, backward])


def reference(diagonal, coupling, start_block, shadow_block):
    block_count = NV // 16
    cell_total = GX * GY * GZ * P_SIZE

    def one_block(position):
        begin_at = (position * 16).astype(jnp.int32)
        start_part = lax.dynamic_slice_in_dim(start_block, begin_at, 16, 4)
        shadow_part = lax.dynamic_slice_in_dim(shadow_block, begin_at, 16, 4)
        stacked = jnp.stack([start_part, shadow_part])
        basis_list = [start_part]
        shadow_list = [shadow_part]
        for step_index in range(STEPS):
            stacked = apply_pair(stacked, diagonal, coupling)
            basis_list.append(stacked[0])
            shadow_list.append(stacked[1])
        moment_part = jnp.einsum('ixyzpn,jxyzpn->ijn', jnp.stack(shadow_list), jnp.stack(basis_list), precision=HIGH) * (1.0 / cell_total)
        return stacked[0], stacked[1], moment_part

    basis_parts, shadow_parts, moment_parts = lax.map(one_block, jnp.arange(block_count, dtype=jnp.int32))
    last_basis = jnp.moveaxis(basis_parts, 0, 4).reshape(GX, GY, GZ, P_SIZE, NV)
    last_shadow = jnp.moveaxis(shadow_parts, 0, 4).reshape(GX, GY, GZ, P_SIZE, NV)
    moments = jnp.moveaxis(moment_parts, 0, 2).reshape(STEPS + 1, STEPS + 1, NV)
    return (last_basis, last_shadow, moments)
```

```python
import functools

import jax
import jax.numpy as jnp
from jax import lax
from jax.experimental import pallas as pl
from jax.experimental.pallas import tpu as pltpu
from jax.sharding import PartitionSpec as P

STEPS = 4
ROWS = 320
FACE = 80
COLS = 128
MESH = pl.DeviceIdType.MESH
F32 = jnp.float32
BF16 = jnp.bfloat16
X_DOWN, Y_DOWN, X_UP, Y_UP = range(4)


def split(x):
    high = x.astype(BF16)
    return high, (x - high.astype(F32)).astype(BF16)


def put_columns(ref, row, x):
    high, low = split(x)
    rows = pl.ds(row, x.shape[0])
    ref[rows, 0:COLS] = high
    ref[rows, COLS:] = low


def put_rows(ref, row, column, below, x):
    high, low = split(x)
    columns = pl.ds(column, x.shape[1])
    ref[pl.ds(row, x.shape[0]), columns] = high
    ref[pl.ds(row + below, x.shape[0]), columns] = low


def product(left, right):
    full = jnp.dot(left, right, preferred_element_type=F32)
    rows = full.shape[0] // 2
    return full[:rows, :COLS] + (full[:rows, COLS:] + full[rows:, :COLS])


def low_half(shape):
    return lax.broadcasted_iota(jnp.int32, shape, len(shape) - 2) < 4


def swap_halves(x):
    return pltpu.roll(x, 4, 1)


def x_trace(u, node):
    return u.reshape(2, 5, 64, COLS)[:, :, node * 16 : node * 16 + 16].reshape(2, FACE, COLS)


def y_low(u):
    parts = u.reshape(20, 4, 8, COLS)
    first, second = parts[:, 0], parts[:, 2]
    return jnp.where(low_half(first.shape), first, swap_halves(second)).reshape(2, FACE, COLS)


def y_high(u):
    parts = u.reshape(20, 4, 8, COLS)
    first, second = parts[:, 1], parts[:, 3]
    return jnp.where(low_half(first.shape), swap_halves(first), second).reshape(2, FACE, COLS)


def scattered(x_lo, y_lo, x_hi, y_hi):
    x_lo = x_lo.reshape(10, 1, 16, COLS)
    x_hi = x_hi.reshape(10, 1, 16, COLS)
    gap = jnp.zeros((10, 1, 32, COLS), F32)
    along_x = jnp.concatenate([x_lo, gap, x_hi], axis=2).reshape(20, 4, 8, COLS)
    y_lo = y_lo.reshape(20, 8, COLS)
    y_hi = y_hi.reshape(20, 8, COLS)
    mask = low_half(y_lo.shape)
    zero = jnp.zeros_like(y_lo)
    along_y = [
        jnp.where(mask, y_lo, zero),
        jnp.where(mask, zero, swap_halves(y_hi)),
        jnp.where(mask, swap_halves(y_lo), zero),
        jnp.where(mask, zero, y_hi),
    ]
    along_y = jnp.concatenate([part[:, None] for part in along_y], axis=1)
    return (along_x + along_y).reshape(2, ROWS, COLS)


def column_sums(x, y):
    return jnp.sum((x * y).reshape(2 * ROWS, COLS), axis=0, keepdims=True)


def kernel(
    sizes,
    scale,
    d_hbm,
    c_hbm,
    b_hbm,
    s_hbm,
    ob_hbm,
    os_hbm,
    om_ref,
    d_in,
    c_in,
    field,
    acc,
    d_pad,
    c_pad,
    z_pad,
    left,
    left_up,
    left_in,
    right,
    right_up,
    right_in,
    sent,
    got,
    sums,
    sums_got,
    load_sem,
    store_sem,
    send_sem,
    recv_sem,
    sums_send,
    sums_recv,
):
    doms, subs, depth = sizes
    heights = doms // depth
    dom, sub = lax.axis_index("dom"), lax.axis_index("sub")
    height, level = dom // depth, lax.rem(dom, depth)

    loads = [
        pltpu.make_async_copy(c_hbm, c_in, load_sem.at[0]),
        pltpu.make_async_copy(b_hbm, field.at[0], load_sem.at[1]),
        pltpu.make_async_copy(s_hbm, field.at[1], load_sem.at[2]),
        pltpu.make_async_copy(d_hbm, d_in, load_sem.at[3]),
    ]
    for load in loads:
        load.start()

    on_sub = lambda by: (dom, lax.rem(sub + by + subs, subs))
    on_dom = lambda by: (lax.rem(dom + by + doms, doms), sub)
    on_level = lambda by: (height * depth + lax.rem(level + by, depth), sub)
    on_height = lambda by: (lax.rem(height + by, heights) * depth + level, sub)
    stages = [
        [on_sub(by) for by in range(1, subs)],
        [on_height(by) for by in range(1, heights)],
        [on_level(by) for by in range(1, depth)],
    ]
    sides = [on_sub(-1), on_dom(-1), on_sub(1), on_dom(1)]
    greeted = [on_dom(-1), on_dom(1)] + stages[0] + stages[1] + stages[2]
    barrier = pltpu.get_barrier_semaphore()
    for peer in greeted:
        pl.semaphore_signal(barrier, inc=1, device_id=peer, device_id_type=MESH)

    for ref in (c_pad, z_pad, d_pad):
        ref[...] = jnp.zeros_like(ref)
    for ref in (left, left_up, left_in, right, right_up, right_in):
        ref[...] = jnp.zeros_like(ref)

    loads[0].wait()
    coupling = c_in[...]
    keep_x = jnp.where(sub == subs - 1, 0.0, 1.0)
    keep_y = jnp.where(dom == doms - 1, 0.0, 1.0)
    c_pad[:, 0, 0:FACE, 0:FACE] = coupling[:, 0] * keep_x
    c_pad[:, 1, 0:FACE, 0:FACE] = coupling[:, 1] * keep_y
    c_pad[:, 2, 0:FACE, 0:FACE] = coupling[:, 2]
    for e in range(2):
        for side in range(2):
            block = c_pad[e, side]
            put_rows(left_in.at[e], side * FACE, side * COLS, 2 * FACE, block[:FACE])
            put_rows(left_up.at[e], side * FACE, side * COLS, 2 * FACE, block.T[:FACE])

    def messages(k, f):
        return [
            pltpu.make_async_remote_copy(
                src_ref=sent.at[k, f, side],
                dst_ref=got.at[k, f, side],
                send_sem=send_sem.at[k, f, side],
                recv_sem=recv_sem.at[k, f, side],
                device_id=peer,
                device_id_type=MESH,
            )
            for side, peer in enumerate(sides)
        ]

    def send_faces(k, f, u):
        copies = messages(k, f)
        sent[k, f, X_DOWN] = x_trace(u, 0)
        copies[X_DOWN].start()
        sent[k, f, Y_DOWN] = y_low(u)
        copies[Y_DOWN].start()
        x_hi, y_hi = x_trace(u, 3), y_high(u)
        for e in range(2):
            put_columns(right_up.at[e], 0, x_hi[e])
            put_columns(right_up.at[e], COLS, y_hi[e])
        for e in range(2):
            up = product(left_up[e], right_up[e])
            sent[k, f, X_UP, e] = up[:FACE]
            sent[k, f, Y_UP, e] = up[FACE:]
        copies[Y_UP].start()
        copies[X_UP].start()

    def local_part(f):
        for e in range(2):
            put_columns(right.at[e], 0, field[f, e])
            put_columns(right.at[e], 384, field[f, 1 - e, pl.ds(3 * e, FACE, stride=4), :])
        for e in range(2):
            acc[f, e] = product(left[f, e], right[e])

    def face_part(k, f):
        for copy in messages(k, f):
            copy.wait_recv()
        for e in range(2):
            put_columns(right_in.at[e], 0, got[k, f, X_DOWN, e])
            put_columns(right_in.at[e], COLS, got[k, f, Y_DOWN, e])
        into = [product(left_in[e], right_in[e]) for e in range(2)]
        x_hi = jnp.concatenate([part[None, :FACE] for part in into], axis=0)
        y_hi = jnp.concatenate([part[None, FACE:] for part in into], axis=0)
        terms = scattered(-got[k, f, X_UP], -got[k, f, Y_UP], x_hi, y_hi)
        return acc[f] + terms if f == 0 else acc[f] - terms

    def total_copies(group, stage):
        first = sum(len(peers) for peers in stages[:stage])
        return [
            pltpu.make_async_remote_copy(
                src_ref=sums.at[group, stage],
                dst_ref=sums_got.at[group, first + i],
                send_sem=sums_send.at[group, first + i],
                recv_sem=sums_recv.at[group, first + i],
                device_id=peer,
                device_id_type=MESH,
            )
            for i, peer in enumerate(stages[stage])
        ]

    def start_total(group, stage):
        for copy in total_copies(group, stage):
            copy.start()

    def end_total(group, stage):
        first = sum(len(peers) for peers in stages[:stage])
        copies = total_copies(group, stage)
        for copy in copies:
            copy.wait_recv()
        total = sums[group, stage]
        for i in range(len(copies)):
            total = total + sums_got[group, first + i]
        sums[group, stage + 1] = total

    pl.semaphore_wait(barrier, len(greeted))

    for f in range(2):
        loads[1 + f].wait()
        send_faces(0, f, field[f])
    sums[...] = jnp.zeros_like(sums)
    sums[0, 0, 0:1] = column_sums(field[1], field[0])

    loads[3].wait()
    z_pad[0, pl.ds(3, FACE, stride=4), :] = c_pad[0, 2, 0:FACE]
    z_pad[1, pl.ds(0, FACE, stride=4), :] = -c_pad[0, 2].T[:FACE]
    for e in range(2):
        d_pad[e, 0:ROWS, 0:ROWS] = d_in[e]
        put_rows(left.at[0, e], 0, 0, ROWS, d_pad[e, 0:ROWS, :])
        put_rows(left.at[0, e], 0, 384, ROWS, z_pad[e])
        put_rows(left.at[1, e], 0, 384, ROWS, -z_pad[e])
        for i in range(3):
            rows = min(COLS, ROWS - i * COLS)
            for j in range(3):
                block = d_pad[e, j * COLS : (j + 1) * COLS, i * COLS : (i + 1) * COLS].T
                put_rows(left.at[1, e], i * COLS, j * COLS, ROWS, block[:rows])
    for f in range(2):
        local_part(f)

    for k in range(STEPS):
        for f in range(2):
            u = face_part(k, f)
            field[f] = u
            if k + 1 < STEPS:
                send_faces(k + 1, f, u)
                local_part(f)
            else:
                pltpu.make_async_copy(field.at[f], (ob_hbm, os_hbm)[f], store_sem.at[f]).start()
            moment = 2 * k + 1 + f
            group, row = (0, moment) if moment < 7 else (1, moment - 7)
            sums[group, 0, row : row + 1] = column_sums(field[1], field[0])
            if moment == 6:
                start_total(0, 0)
            if moment == 7:
                end_total(0, 0)
                start_total(0, 1)
    start_total(1, 0)
    end_total(0, 1)
    start_total(0, 2)
    end_total(1, 0)
    start_total(1, 1)
    end_total(0, 2)
    end_total(1, 1)
    start_total(1, 2)
    end_total(1, 2)
    early, late = sums[0, 3] * scale, sums[1, 3] * scale
    rows = [early[i : i + 1] for i in range(7)] + [late[i : i + 1] for i in range(2)]
    for i in range(STEPS + 1):
        for j in range(STEPS + 1):
            om_ref[i, j : j + 1] = rows[i + j]

    for k in range(STEPS):
        for f in range(2):
            for copy in messages(k, f):
                copy.wait_send()
    for group in range(2):
        for stage in range(3):
            for copy in total_copies(group, stage):
                copy.wait_send()
    for f in range(2):
        pltpu.make_async_copy(field.at[f], (ob_hbm, os_hbm)[f], store_sem.at[f]).wait()


def solution(mesh):
    doms, subs = mesh.shape["dom"], mesh.shape["sub"]
    depth = 12 if doms % 12 == 0 else 1
    peers = (subs - 1) + (doms // depth - 1) + (depth - 1)

    def body(diagonal, coupling, start_block, shadow_block):
        count = 2 * ROWS * doms * subs
        moments_shape = (STEPS + 1, STEPS + 1, COLS)
        field_shape = jax.ShapeDtypeStruct((2, ROWS, COLS), F32)
        outs = pl.pallas_call(
            functools.partial(kernel, (doms, subs, depth), 1.0 / count),
            out_shape=(field_shape, field_shape, jax.ShapeDtypeStruct(moments_shape, F32)),
            in_specs=[pl.BlockSpec(memory_space=pltpu.HBM)] * 4,
            out_specs=(
                pl.BlockSpec(memory_space=pltpu.HBM),
                pl.BlockSpec(memory_space=pltpu.HBM),
                pl.BlockSpec(memory_space=pltpu.VMEM),
            ),
            scratch_shapes=[
                pltpu.VMEM((2, ROWS, ROWS), F32),
                pltpu.VMEM((2, 3, FACE, FACE), F32),
                pltpu.VMEM((2, 2, ROWS, COLS), F32),
                pltpu.VMEM((2, 2, ROWS, COLS), F32),
                pltpu.VMEM((2, 384, 384), F32),
                pltpu.VMEM((2, 3, COLS, COLS), F32),
                pltpu.VMEM((2, ROWS, COLS), F32),
                pltpu.VMEM((2, 2, 2 * ROWS, 512), BF16),
                pltpu.VMEM((2, 4 * FACE, 256), BF16),
                pltpu.VMEM((2, 4 * FACE, 256), BF16),
                pltpu.VMEM((2, 512, 256), BF16),
                pltpu.VMEM((2, 256, 256), BF16),
                pltpu.VMEM((2, 256, 256), BF16),
                pltpu.VMEM((STEPS, 2, 4, 2, FACE, COLS), F32),
                pltpu.VMEM((STEPS, 2, 4, 2, FACE, COLS), F32),
                pltpu.VMEM((2, 4, 8, COLS), F32),
                pltpu.VMEM((2, peers, 8, COLS), F32),
                pltpu.SemaphoreType.DMA((4,)),
                pltpu.SemaphoreType.DMA((2,)),
                pltpu.SemaphoreType.DMA((STEPS, 2, 4)),
                pltpu.SemaphoreType.DMA((STEPS, 2, 4)),
                pltpu.SemaphoreType.DMA((2, peers)),
                pltpu.SemaphoreType.DMA((2, peers)),
            ],
            compiler_params=pltpu.CompilerParams(
                collective_id=0, has_side_effects=True, vmem_limit_bytes=40 * 1024 * 1024
            ),
            name="powers",
        )(
            diagonal.reshape(2, ROWS, ROWS),
            coupling.reshape(2, 3, FACE, FACE),
            start_block.reshape(2, ROWS, COLS),
            shadow_block.reshape(2, ROWS, COLS),
        )
        shape = start_block.shape
        return outs[0].reshape(shape), outs[1].reshape(shape), outs[2]

    placed = P("sub", "dom", None, None, None)
    return jax.shard_map(
        body,
        mesh=mesh,
        in_specs=(placed, P("sub", "dom", None, None, None, None), placed, placed),
        out_specs=(placed, placed, P()),
        check_vma=False,
    )
```

```python
import functools

import jax
import jax.numpy as jnp
from jax import lax
from jax.experimental import pallas as pl
from jax.experimental.pallas import tpu as pltpu
from jax.sharding import PartitionSpec as P

STEPS = 4
ROWS = 320
FACE = 80
COLS = 128
MESH = pl.DeviceIdType.MESH
F32 = jnp.float32
BF16 = jnp.bfloat16
X_DOWN, Y_DOWN, X_UP, Y_UP = range(4)
TOKENS = 6
SUMS = 2 * STEPS + 1


def split(x):
    high = x.astype(BF16)
    return high, (x - high.astype(F32)).astype(BF16)


def put_columns(ref, row, x):
    high, low = split(x)
    rows = pl.ds(row, x.shape[0])
    ref[rows, 0:COLS] = high
    ref[rows, COLS:] = low


def put_rows(ref, row, column, below, x):
    high, low = split(x)
    columns = pl.ds(column, x.shape[1])
    ref[pl.ds(row, x.shape[0]), columns] = high
    ref[pl.ds(row + below, x.shape[0]), columns] = low


def product(left, right):
    full = jnp.dot(left, right, preferred_element_type=F32)
    rows = full.shape[0] // 2
    return full[:rows, :COLS] + (full[:rows, COLS:] + full[rows:, :COLS])


def x_face(ref, node):
    return ref[:, :, node * 16 : node * 16 + 16].reshape(2, FACE, COLS)


def low_half(shape):
    return lax.broadcasted_iota(jnp.int32, shape, len(shape) - 2) < 4


def swap_halves(x):
    return pltpu.roll(x, 4, 1)


def y_parts(u):
    parts = u.reshape(20, 4, 8, COLS)
    return [parts[:, i] for i in range(4)]


def y_low(u):
    first, _, second, _ = y_parts(u)
    return jnp.where(low_half(first.shape), first, swap_halves(second)).reshape(2, FACE, COLS)


def y_high(u):
    _, first, _, second = y_parts(u)
    return jnp.where(low_half(first.shape), swap_halves(first), second).reshape(2, FACE, COLS)


def add_y(u, low, high):
    parts = y_parts(u)
    low, high = low.reshape(20, 8, COLS), high.reshape(20, 8, COLS)
    mask = low_half(low.shape)
    zero = jnp.zeros_like(low)
    terms = [
        jnp.where(mask, low, zero),
        jnp.where(mask, zero, swap_halves(high)),
        jnp.where(mask, swap_halves(low), zero),
        jnp.where(mask, zero, high),
    ]
    whole = jnp.concatenate([(part + term)[:, None] for part, term in zip(parts, terms)], axis=1)
    return whole.reshape(2, 5, 64, COLS)


def column_sums(x, y):
    return jnp.sum((x * y).reshape(2 * ROWS, COLS), axis=0, keepdims=True)


def far_first(count):
    return sorted(range(1, count), key=lambda by: -min(by, count - by))


def kernel(
    sizes,
    d_hbm,
    c_hbm,
    b_hbm,
    s_hbm,
    ob_hbm,
    os_hbm,
    total_ref,
    d_in,
    c_in,
    field,
    acc,
    d_pad,
    c_pad,
    z_pad,
    left,
    left_up,
    left_in,
    right,
    right_up,
    right_in,
    sent,
    got,
    sums,
    sums_got,
    load_sem,
    store_sem,
    send_sem,
    recv_sem,
    sums_send,
    sums_recv,
    token_sem,
):
    doms, subs, depth = sizes
    heights, chips = doms // depth, subs // 2
    dom, sub = lax.axis_index("dom"), lax.axis_index("sub")
    height, level = dom // depth, lax.rem(dom, depth)
    chip, core = sub // 2, lax.rem(sub, 2)

    loads = [
        pltpu.make_async_copy(b_hbm, field.at[0], load_sem.at[0]),
        pltpu.make_async_copy(c_hbm, c_in, load_sem.at[1]),
        pltpu.make_async_copy(s_hbm, field.at[1], load_sem.at[2]),
        pltpu.make_async_copy(d_hbm, d_in, load_sem.at[3]),
    ]
    for load in loads:
        load.start()

    def on_sub(by):
        return dom, lax.rem(sub + by + subs, subs)

    def on_dom(by):
        return lax.rem(dom + by + doms, doms), sub

    def on_level(by, to=sub):
        return height * depth + lax.rem(level + by + depth, depth), to

    def on_height(by):
        return lax.rem(height + by + heights, heights) * depth + level, sub

    def on_chip(by, to):
        return dom, lax.rem(chip + by, chips) * 2 + to

    sides = [on_sub(-1), on_dom(-1), on_sub(1), on_dom(1)]
    near = [on_level(-1), on_level(1), on_height(-1), on_height(1)]
    barrier = pltpu.get_barrier_semaphore()
    for peer in sides + near:
        pl.semaphore_signal(barrier, inc=1, device_id=peer, device_id_type=MESH)

    def pass_token(step):
        for peer in near:
            pl.semaphore_signal(token_sem.at[step], inc=1, device_id=peer, device_id_type=MESH)

    def message(k, f, side):
        return pltpu.make_async_remote_copy(
            src_ref=sent.at[k, f, side],
            dst_ref=got.at[k, f, side],
            send_sem=send_sem.at[k, f, side],
            recv_sem=recv_sem.at[k, f, side],
            device_id=sides[side],
            device_id_type=MESH,
        )

    def through(lefts, side, rights, x):
        for e in range(2):
            put_columns(rights.at[side, e], 0, x[e])
        parts = [product(lefts[side, e], rights[side, e]) for e in range(2)]
        return jnp.concatenate([part[None] for part in parts], axis=0)

    for ref in (c_pad, right_up, right_in):
        ref[...] = jnp.zeros_like(ref)

    loads[0].wait()
    sent[0, 0, Y_DOWN] = y_low(field[0])
    sent[0, 0, X_DOWN] = x_face(field.at[0], 0)
    pl.semaphore_wait(barrier, len(sides + near))
    message(0, 0, Y_DOWN).start()
    message(0, 0, X_DOWN).start()
    pass_token(0)

    loads[1].wait()
    for e in range(2):
        for side, last in enumerate((sub == subs - 1, dom == doms - 1)):
            c_pad[e, side, 0:FACE, 0:FACE] = jnp.where(last, 0.0, c_in[e, side])
        c_pad[e, 2, 0:FACE, 0:FACE] = c_in[e, 2]
    for side in (1, 0):
        for e in range(2):
            put_rows(left_up.at[side, e], 0, 0, FACE, c_pad[e, side].T[:FACE])

    def send_up(k, f, side, trace):
        sent[k, f, X_UP + side] = through(left_up, side, right_up, trace)
        message(k, f, X_UP + side).start()

    send_up(0, 0, 1, y_high(field[0]))
    send_up(0, 0, 0, x_face(field.at[0], 3))
    loads[2].wait()
    sent[0, 1, Y_DOWN] = y_low(field[1])
    message(0, 1, Y_DOWN).start()
    send_up(0, 1, 1, y_high(field[1]))
    sent[0, 1, X_DOWN] = x_face(field.at[1], 0)
    message(0, 1, X_DOWN).start()
    send_up(0, 1, 0, x_face(field.at[1], 3))

    for side in range(2):
        for e in range(2):
            put_rows(left_in.at[side, e], 0, 0, FACE, c_pad[e, side, 0:FACE])
    for ref in (z_pad, d_pad, left, right):
        ref[...] = jnp.zeros_like(ref)
    z_pad[0, pl.ds(3, FACE, stride=4), :] = c_pad[0, 2, 0:FACE]
    z_pad[1, pl.ds(0, FACE, stride=4), :] = -c_pad[0, 2].T[:FACE]
    loads[3].wait()
    for e in range(2):
        d_pad[e, 0:ROWS, 0:ROWS] = d_in[e]
        put_rows(left.at[0, e], 0, 0, ROWS, d_pad[e, 0:ROWS, :])
        put_rows(left.at[0, e], 0, 384, ROWS, z_pad[e])
        put_rows(left.at[1, e], 0, 384, ROWS, -z_pad[e])
        for i in range(3):
            rows = min(COLS, ROWS - i * COLS)
            for j in range(3):
                block = d_pad[e, j * COLS : (j + 1) * COLS, i * COLS : (i + 1) * COLS].T
                put_rows(left.at[1, e], i * COLS, j * COLS, ROWS, block[:rows])

    def local_part(f):
        flat = field.at[f].reshape(2, ROWS, COLS)
        for e in range(2):
            put_columns(right.at[e], 0, flat[e])
            put_columns(right.at[e], 384, flat[1 - e, pl.ds(3 * e, FACE, stride=4), :])
        for e in range(2):
            acc[f, e] = product(left[f, e], right[e]).reshape(5, 64, COLS)

    for f in range(2):
        local_part(f)
    sums[0, 0:1] = column_sums(field[1], field[0])

    for k in range(STEPS):
        for f in range(2):
            more = k + 1 < STEPS
            sign = 1.0 - 2.0 * f
            message(k, f, X_UP).wait_recv()
            message(k, f, X_DOWN).wait_recv()
            into = through(left_in, 0, right_in, got[k, f, X_DOWN]).reshape(2, 5, 16, COLS)
            acc[f, :, :, 48:64] = acc[f, :, :, 48:64] + sign * into
            from_below = got[k, f, X_UP].reshape(2, 5, 16, COLS)
            acc[f, :, :, 0:16] = acc[f, :, :, 0:16] - sign * from_below
            u = acc[f]
            message(k, f, Y_UP).wait_recv()
            low = -sign * got[k, f, Y_UP]
            if more:
                sent[k + 1, f, Y_DOWN] = y_low(u) + low
                message(k + 1, f, Y_DOWN).start()
            message(k, f, Y_DOWN).wait_recv()
            high = sign * through(left_in, 1, right_in, got[k, f, Y_DOWN])
            if more:
                send_up(k + 1, f, 1, y_high(u) + high)
            field[f] = add_y(u, low, high)
            if more:
                sent[k + 1, f, X_DOWN] = x_face(field.at[f], 0)
                message(k + 1, f, X_DOWN).start()
                send_up(k + 1, f, 0, x_face(field.at[f], 3))
                local_part(f)
            else:
                pltpu.make_async_copy(field.at[f], (ob_hbm, os_hbm)[f], store_sem.at[f]).start()
            moment = 2 * k + 1 + f
            sums[0, moment : moment + 1] = column_sums(field[1], field[0])
            step = 2 * k + f
            if step < TOKENS:
                pl.semaphore_wait(token_sem.at[step], len(near))
                if step + 1 < TOKENS:
                    pass_token(step + 1)

    def total_copy(stage, slot, peer, send=None):
        return pltpu.make_async_remote_copy(
            src_ref=sums.at[stage],
            dst_ref=sums_got.at[slot],
            send_sem=sums_send.at[slot if send is None else send],
            recv_sem=sums_recv.at[slot],
            device_id=peer,
            device_id_type=MESH,
        )

    def arrived(total, stage, first, count):
        for slot in range(first, first + count):
            total_copy(stage, slot, on_level(1)).wait_recv()
            total = total + sums_got[slot]
        return total

    inner, outer = on_chip(0, 0), on_chip(0, 1)
    across = far_first(chips)
    slot_in, slot_y = 2 * len(across), 2 * len(across) + 1
    slot_z = slot_y + heights - 1
    slot_out = slot_z + depth - 1

    @pl.when(core == 0)
    def _():
        copies = [total_copy(0, i, on_chip(by, 1)) for i, by in enumerate(across)]
        copies.append(total_copy(0, slot_in, outer))
        for copy in copies:
            copy.start()
        total_copy(2, slot_out, outer).wait_recv()
        total_ref[...] = arrived(sums_got[slot_out], 2, slot_z, depth - 1)
        for copy in copies:
            copy.wait_send()

    @pl.when(core == 1)
    def _():
        copies = [total_copy(0, len(across) + i, on_chip(by, 1)) for i, by in enumerate(across)]
        for copy in copies:
            copy.start()
        sums[1] = arrived(sums[0], 0, 0, slot_y)
        along_y = [total_copy(1, slot_y + i, on_height(by)) for i, by in enumerate(far_first(heights))]
        for copy in along_y:
            copy.start()
        sums[2] = arrived(sums[1], 1, slot_y, heights - 1)
        along_z = []
        for i, by in enumerate(far_first(depth)):
            along_z.append(total_copy(2, slot_z + i, on_level(by, chip * 2), slot_out + 1 + i))
            along_z.append(total_copy(2, slot_z + i, on_level(by)))
        along_z.append(total_copy(2, slot_out, inner))
        for copy in along_z:
            copy.start()
        total_ref[...] = arrived(sums[2], 2, slot_z, depth - 1)
        for copy in copies + along_y + along_z:
            copy.wait_send()

    for k in range(STEPS):
        for f in range(2):
            for side in range(4):
                message(k, f, side).wait_send()
    for f in range(2):
        pltpu.make_async_copy(field.at[f], (ob_hbm, os_hbm)[f], store_sem.at[f]).wait()


def pin(x):
    return pltpu.with_memory_space_constraint(x, pltpu.HBM)


def finish(scale, b_hbm, s_hbm, total_ref, ob_hbm, os_hbm, moments_ref, sem):
    copies = [
        pltpu.make_async_copy(b_hbm, ob_hbm, sem.at[0]),
        pltpu.make_async_copy(s_hbm, os_hbm, sem.at[1]),
    ]
    for copy in copies:
        copy.start()
    total = total_ref[...] * scale
    for i in range(STEPS + 1):
        moments_ref[i] = total[i : i + STEPS + 1]
    for copy in copies:
        copy.wait()


def solution(mesh):
    doms, subs = mesh.shape["dom"], mesh.shape["sub"]
    depth = 12
    slots = 2 * (subs // 2 - 1) + 1 + (doms // depth - 1) + (depth - 1) + 1
    anywhere = pl.BlockSpec(memory_space=pl.ANY)
    inside = pl.BlockSpec(memory_space=pltpu.VMEM)
    grant = 40 * 1024 * 1024

    def body(diagonal, coupling, start_block, shadow_block):
        count = 2 * ROWS * doms * subs
        field_shape = jax.ShapeDtypeStruct((2, 5, 64, COLS), F32)
        moments_shape = jax.ShapeDtypeStruct((STEPS + 1, STEPS + 1, COLS), F32)
        total_shape = jax.ShapeDtypeStruct((SUMS, COLS), F32)
        powers = pl.pallas_call(
            functools.partial(kernel, (doms, subs, depth)),
            out_shape=(field_shape, field_shape, total_shape),
            in_specs=[anywhere] * 4,
            out_specs=(anywhere, anywhere, inside),
            scratch_shapes=[
                pltpu.VMEM((2, ROWS, ROWS), F32),
                pltpu.VMEM((2, 3, FACE, FACE), F32),
                pltpu.VMEM((2, 2, 5, 64, COLS), F32),
                pltpu.VMEM((2, 2, 5, 64, COLS), F32),
                pltpu.VMEM((2, 384, 384), F32),
                pltpu.VMEM((2, 3, COLS, COLS), F32),
                pltpu.VMEM((2, ROWS, COLS), F32),
                pltpu.VMEM((2, 2, 2 * ROWS, 512), BF16),
                pltpu.VMEM((2, 2, 2 * FACE, COLS), BF16),
                pltpu.VMEM((2, 2, 2 * FACE, COLS), BF16),
                pltpu.VMEM((2, 512, 256), BF16),
                pltpu.VMEM((2, 2, COLS, 256), BF16),
                pltpu.VMEM((2, 2, COLS, 256), BF16),
                pltpu.VMEM((STEPS, 2, 4, 2, FACE, COLS), F32),
                pltpu.VMEM((STEPS, 2, 4, 2, FACE, COLS), F32),
                pltpu.VMEM((3, SUMS, COLS), F32),
                pltpu.VMEM((slots, SUMS, COLS), F32),
                pltpu.SemaphoreType.DMA((4,)),
                pltpu.SemaphoreType.DMA((2,)),
                pltpu.SemaphoreType.DMA((STEPS, 2, 4)),
                pltpu.SemaphoreType.DMA((STEPS, 2, 4)),
                pltpu.SemaphoreType.DMA((slots + depth - 1,)),
                pltpu.SemaphoreType.DMA((slots,)),
                pltpu.SemaphoreType.REGULAR((TOKENS,)),
            ],
            compiler_params=pltpu.CompilerParams(
                collective_id=0, has_side_effects=True, vmem_limit_bytes=grant
            ),
            name="powers",
        )(
            pin(diagonal.reshape(2, ROWS, ROWS)),
            pin(coupling.reshape(2, 3, FACE, FACE)),
            pin(start_block.reshape(2, 5, 64, COLS)),
            pin(shadow_block.reshape(2, 5, 64, COLS)),
        )
        basis, shadow, moments = pl.pallas_call(
            functools.partial(finish, 1.0 / count),
            out_shape=(field_shape, field_shape, moments_shape),
            in_specs=[anywhere, anywhere, inside],
            out_specs=(anywhere, anywhere, inside),
            scratch_shapes=[pltpu.SemaphoreType.DMA((2,))],
            compiler_params=pltpu.CompilerParams(vmem_limit_bytes=grant),
            name="finish",
        )(*powers)
        return basis.reshape(start_block.shape), shadow.reshape(start_block.shape), moments

    placed = P("sub", "dom", None, None, None)
    return jax.shard_map(
        body,
        mesh=mesh,
        in_specs=(placed, P("sub", "dom", None, None, None, None), placed, placed),
        out_specs=(placed, placed, P()),
        check_vma=False,
    )
```

```python
import functools

import jax
import jax.numpy as jnp
from jax import lax
from jax.experimental import pallas as pl
from jax.experimental.pallas import tpu as pltpu
from jax.sharding import PartitionSpec as P

STEPS = 4
ROWS = 320
FACE = 80
COLS = 128
MESH = pl.DeviceIdType.MESH
F32 = jnp.float32
BF16 = jnp.bfloat16
DOWN, UP = range(2)
TOKENS = 6
SUMS = 2 * STEPS + 1


def split(x):
    high = x.astype(BF16)
    return high, (x - high.astype(F32)).astype(BF16)


def put_columns(ref, row, x):
    high, low = split(x)
    rows = pl.ds(row, x.shape[0])
    ref[rows, 0:COLS] = high
    ref[rows, COLS:] = low


def put_rows(ref, row, column, below, x):
    high, low = split(x)
    columns = pl.ds(column, x.shape[1])
    ref[pl.ds(row, x.shape[0]), columns] = high
    ref[pl.ds(row + below, x.shape[0]), columns] = low


def product(left, right):
    full = jnp.dot(left, right, preferred_element_type=F32)
    rows = full.shape[0] // 2
    return full[:rows, :COLS] + (full[:rows, COLS:] + full[rows:, :COLS])


def x_face(ref, node):
    return ref[:, :, node * 16 : node * 16 + 16].reshape(2, FACE, COLS)


def low_half(shape):
    return lax.broadcasted_iota(jnp.int32, shape, len(shape) - 2) < 4


def swap_halves(x):
    return pltpu.roll(x, 4, 1)


def y_parts(u):
    parts = u.reshape(10, 4, 8, COLS)
    return [parts[:, i] for i in range(4)]


def y_low(u):
    first, _, second, _ = y_parts(u)
    return jnp.where(low_half(first.shape), first, swap_halves(second)).reshape(FACE, COLS)


def y_high(u):
    _, first, _, second = y_parts(u)
    return jnp.where(low_half(first.shape), swap_halves(first), second).reshape(FACE, COLS)


def add_y(u, low, high):
    parts = y_parts(u)
    low, high = low.reshape(10, 8, COLS), high.reshape(10, 8, COLS)
    mask = low_half(low.shape)
    zero = jnp.zeros_like(low)
    terms = [
        jnp.where(mask, low, zero),
        jnp.where(mask, zero, swap_halves(high)),
        jnp.where(mask, swap_halves(low), zero),
        jnp.where(mask, zero, high),
    ]
    whole = jnp.concatenate([(part + term)[:, None] for part, term in zip(parts, terms)], axis=1)
    return whole.reshape(5, 64, COLS)


def column_sums(x, y):
    return jnp.sum((x * y).reshape(2 * ROWS, COLS), axis=0, keepdims=True)


def far_first(count):
    return sorted(range(1, count), key=lambda by: -min(by, count - by))


def kernel(
    sizes,
    d_hbm,
    c_hbm,
    b_hbm,
    s_hbm,
    ob_hbm,
    os_hbm,
    total_ref,
    d_in,
    c_in,
    field,
    acc,
    d_pad,
    c_pad,
    z_pad,
    left,
    left_up,
    left_in,
    left_y,
    right,
    right_up,
    right_in,
    right_y,
    x_sent,
    x_got,
    y_sent,
    y_got,
    sums,
    sums_got,
    load_sem,
    store_sem,
    x_send,
    x_recv,
    y_send,
    y_recv,
    sums_send,
    sums_recv,
    token_sem,
):
    doms, subs, depth = sizes
    heights, chips = doms // depth, subs // 2
    dom, sub = lax.axis_index("dom"), lax.axis_index("sub")
    height, level = dom // depth, lax.rem(dom, depth)
    chip, core = sub // 2, lax.rem(sub, 2)

    loads = [
        pltpu.make_async_copy(b_hbm, field.at[0], load_sem.at[0]),
        pltpu.make_async_copy(s_hbm, field.at[1], load_sem.at[1]),
        pltpu.make_async_copy(c_hbm, c_in, load_sem.at[2]),
        pltpu.make_async_copy(d_hbm, d_in, load_sem.at[3]),
    ]
    loads[0].start()

    def on_sub(by):
        return dom, lax.rem(sub + by + subs, subs)

    def on_dom(by):
        return lax.rem(dom + by + doms, doms), sub

    def on_level(by, to=sub):
        return height * depth + lax.rem(level + by + depth, depth), to

    def on_height(by):
        return lax.rem(height + by + heights, heights) * depth + level, sub

    def on_chip(by, to):
        return dom, lax.rem(chip + by, chips) * 2 + to

    near = [on_level(-1), on_level(1), on_height(-1), on_height(1)]
    greeted = [on_dom(-1), on_dom(1), on_sub(-1), on_sub(1)] + near
    barrier = pltpu.get_barrier_semaphore()
    for peer in greeted:
        pl.semaphore_signal(barrier, inc=1, device_id=peer, device_id_type=MESH)

    for load in loads[1:]:
        load.start()

    def pass_token(step):
        for peer in near:
            pl.semaphore_signal(token_sem.at[step], inc=1, device_id=peer, device_id_type=MESH)

    def x_message(k, f, way):
        return pltpu.make_async_remote_copy(
            src_ref=x_sent.at[k, f, way],
            dst_ref=x_got.at[k, f, way],
            send_sem=x_send.at[k, f, way],
            recv_sem=x_recv.at[k, f, way],
            device_id=on_sub(2 * way - 1),
            device_id_type=MESH,
        )

    def y_message(k, f, way, e):
        return pltpu.make_async_remote_copy(
            src_ref=y_sent.at[k, f, way, e],
            dst_ref=y_got.at[k, f, way, e],
            send_sem=y_send.at[k, f, way, e],
            recv_sem=y_recv.at[k, f, way, e],
            device_id=on_dom(2 * way - 1),
            device_id_type=MESH,
        )

    def through(lefts, e, rights, x):
        put_columns(rights.at[e], 0, x)
        return product(lefts[e], rights[e])

    def y_down(k, f, e, trace):
        y_sent[k, f, DOWN, e] = trace
        y_message(k, f, DOWN, e).start()

    def y_up(k, f, e):
        y_sent[k, f, UP, e] = product(left_y[e], right_y[e])
        y_message(k, f, UP, e).start()

    def x_down(k, f):
        x_sent[k, f, DOWN] = x_face(field.at[f], 0)
        x_message(k, f, DOWN).start()

    def x_up(k, f):
        trace = x_face(field.at[f], 3)
        for e in range(2):
            x_sent[k, f, UP, e] = through(left_up, e, right_up, trace[e])
        x_message(k, f, UP).start()

    for ref in (c_pad, right_up, right_in, left_y, right_y):
        ref[...] = jnp.zeros_like(ref)

    loads[0].wait()
    for e in range(2):
        y_sent[0, 0, DOWN, e] = y_low(field[0, e])
    x_sent[0, 0, DOWN] = x_face(field.at[0], 0)
    pl.semaphore_wait(barrier, len(greeted))
    for e in range(2):
        y_message(0, 0, DOWN, e).start()
    x_message(0, 0, DOWN).start()
    pass_token(0)
    loads[1].wait()
    for e in range(2):
        y_down(0, 1, e, y_low(field[1, e]))
    x_down(0, 1)

    loads[2].wait()
    for e in range(2):
        for side, last in enumerate((sub == subs - 1, dom == doms - 1)):
            c_pad[e, side, 0:FACE, 0:FACE] = jnp.where(last, 0.0, c_in[e, side])
        c_pad[e, 2, 0:FACE, 0:FACE] = c_in[e, 2]
    for e in range(2):
        put_rows(left_y.at[e], 0, 0, FACE, c_pad[e, 1].T[:FACE])
    for f in range(2):
        for e in range(2):
            put_columns(right_y.at[e], 0, y_high(field[f, e]))
            y_up(0, f, e)
    for e in range(2):
        put_rows(left_up.at[e], 0, 0, FACE, c_pad[e, 0].T[:FACE])
    for f in range(2):
        x_up(0, f)

    for side in range(2):
        for e in range(2):
            put_rows(left_in.at[side, e], 0, 0, FACE, c_pad[e, side, 0:FACE])
    for e in range(2):
        put_columns(right_in.at[e], 0, c_pad[e, 1, 0:FACE])
        put_rows(left_y.at[e], 0, COLS, FACE, product(left_y[e, :, 0:COLS], right_in[e]))
    for ref in (z_pad, d_pad, left, right):
        ref[...] = jnp.zeros_like(ref)
    z_pad[0, pl.ds(3, FACE, stride=4), :] = c_pad[0, 2, 0:FACE]
    z_pad[1, pl.ds(0, FACE, stride=4), :] = -c_pad[0, 2].T[:FACE]
    loads[3].wait()
    for e in range(2):
        d_pad[e, 0:ROWS, 0:ROWS] = d_in[e]
        put_rows(left.at[0, e], 0, 0, ROWS, d_pad[e, 0:ROWS, :])
        put_rows(left.at[0, e], 0, 384, ROWS, z_pad[e])
        put_rows(left.at[1, e], 0, 384, ROWS, -z_pad[e])
        for i in range(3):
            rows = min(COLS, ROWS - i * COLS)
            for j in range(3):
                block = d_pad[e, j * COLS : (j + 1) * COLS, i * COLS : (i + 1) * COLS].T
                put_rows(left.at[1, e], i * COLS, j * COLS, ROWS, block[:rows])

    def local_part(f):
        flat = field.at[f].reshape(2, ROWS, COLS)
        for e in range(2):
            put_columns(right.at[e], 0, flat[e])
            put_columns(right.at[e], 384, flat[1 - e, pl.ds(3 * e, FACE, stride=4), :])
        for e in range(2):
            acc[f, e] = product(left[f, e], right[e]).reshape(5, 64, COLS)

    for f in range(2):
        local_part(f)
    sums[0, 0:1] = column_sums(field[1], field[0])

    for k in range(STEPS):
        more = k + 1 < STEPS
        for f in range(2):
            sign = 1.0 - 2.0 * f
            for way in (UP, DOWN):
                x_message(k, f, way).wait_recv()
            for e in range(2):
                into = through(left_in.at[0], e, right_in, x_got[k, f, DOWN, e]).reshape(5, 16, COLS)
                acc[f, e, :, 48:64] = acc[f, e, :, 48:64] + sign * into
                back = x_got[k, f, UP, e].reshape(5, 16, COLS)
                acc[f, e, :, 0:16] = acc[f, e, :, 0:16] - sign * back
            if more:
                for e in range(2):
                    put_columns(right_y.at[e], 0, y_high(acc[f, e]))

            def from_above(e):
                y_message(k, f, DOWN, e).wait_recv()
                put_columns(right_y.at[e], COLS, sign * y_got[k, f, DOWN, e])
                if more:
                    y_up(k + 1, f, e)

            def from_below(e):
                y_message(k, f, UP, e).wait_recv()
                if more:
                    y_down(k + 1, f, e, y_low(acc[f, e]) - sign * y_got[k, f, UP, e])

            for e in range(2):
                from_below(e)
                from_above(e)
            for e in range(2):
                high = product(left_in[1, e], right_y[e, COLS:])
                field[f, e] = add_y(acc[f, e], -sign * y_got[k, f, UP, e], high)
            if more:
                x_down(k + 1, f)
                x_up(k + 1, f)
            else:
                pltpu.make_async_copy(field.at[f], (ob_hbm, os_hbm)[f], store_sem.at[f]).start()
            moment = 2 * k + 1 + f
            sums[0, moment : moment + 1] = column_sums(field[1], field[0])
            step = 2 * k + f
            if step < TOKENS:
                pl.semaphore_wait(token_sem.at[step], len(near))
                if step + 1 < TOKENS:
                    pass_token(step + 1)
            if more and f == 1:
                local_part(0)
                local_part(1)

    def total_copy(stage, slot, peer, send=None):
        return pltpu.make_async_remote_copy(
            src_ref=sums.at[stage],
            dst_ref=sums_got.at[slot],
            send_sem=sums_send.at[slot if send is None else send],
            recv_sem=sums_recv.at[slot],
            device_id=peer,
            device_id_type=MESH,
        )

    def arrived(total, stage, first, count):
        for slot in range(first, first + count):
            total_copy(stage, slot, on_level(1)).wait_recv()
            total = total + sums_got[slot]
        return total

    inner, outer = on_chip(0, 0), on_chip(0, 1)
    across = far_first(chips)
    slot_in, slot_y = 2 * len(across), 2 * len(across) + 1
    slot_z = slot_y + heights - 1
    slot_out = slot_z + depth - 1

    @pl.when(core == 0)
    def _():
        copies = [total_copy(0, i, on_chip(by, 1)) for i, by in enumerate(across)]
        copies.append(total_copy(0, slot_in, outer))
        for copy in copies:
            copy.start()
        total_copy(2, slot_out, outer).wait_recv()
        total_ref[...] = arrived(sums_got[slot_out], 2, slot_z, depth - 1)
        for copy in copies:
            copy.wait_send()

    @pl.when(core == 1)
    def _():
        copies = [total_copy(0, len(across) + i, on_chip(by, 1)) for i, by in enumerate(across)]
        for copy in copies:
            copy.start()
        sums[1] = arrived(sums[0], 0, 0, slot_y)
        along_y = [total_copy(1, slot_y + i, on_height(by)) for i, by in enumerate(far_first(heights))]
        for copy in along_y:
            copy.start()
        sums[2] = arrived(sums[1], 1, slot_y, heights - 1)
        along_z = []
        for i in range(depth - 1):
            after = (i + depth - level) // depth
            place = height * depth + i + after
            slot = slot_z + level - 1 + after
            along_z.append(total_copy(2, slot, (place, chip * 2), slot_z + i))
            along_z.append(total_copy(2, slot, (place, sub), slot_out + 1 + i))
        along_z.append(total_copy(2, slot_out, inner))
        for copy in along_z:
            copy.start()
        total_ref[...] = arrived(sums[2], 2, slot_z, depth - 1)
        for copy in copies + along_y + along_z:
            copy.wait_send()

    for k in range(STEPS):
        for f in range(2):
            for way in range(2):
                x_message(k, f, way).wait_send()
                for e in range(2):
                    y_message(k, f, way, e).wait_send()
    for f in range(2):
        pltpu.make_async_copy(field.at[f], (ob_hbm, os_hbm)[f], store_sem.at[f]).wait()


def pin(x):
    return pltpu.with_memory_space_constraint(x, pltpu.HBM)


def finish(scale, b_hbm, s_hbm, total_ref, ob_hbm, os_hbm, moments_ref, sem):
    copies = [
        pltpu.make_async_copy(b_hbm.at[e], ob_hbm.at[e], sem.at[0, e]) for e in range(2)
    ] + [pltpu.make_async_copy(s_hbm.at[e], os_hbm.at[e], sem.at[1, e]) for e in range(2)]
    for copy in copies:
        copy.start()
    total = total_ref[...] * scale
    for i in range(STEPS + 1):
        moments_ref[i] = total[i : i + STEPS + 1]
    for copy in copies:
        copy.wait()


def solution(mesh):
    doms, subs = mesh.shape["dom"], mesh.shape["sub"]
    depth = 12
    slots = 2 * (subs // 2 - 1) + 1 + (doms // depth - 1) + (depth - 1) + 1
    anywhere = pl.BlockSpec(memory_space=pl.ANY)
    inside = pl.BlockSpec(memory_space=pltpu.VMEM)
    grant = 40 * 1024 * 1024

    def body(diagonal, coupling, start_block, shadow_block):
        count = 2 * ROWS * doms * subs
        field_shape = jax.ShapeDtypeStruct((2, 5, 64, COLS), F32)
        moments_shape = jax.ShapeDtypeStruct((STEPS + 1, STEPS + 1, COLS), F32)
        total_shape = jax.ShapeDtypeStruct((SUMS, COLS), F32)
        powers = pl.pallas_call(
            functools.partial(kernel, (doms, subs, depth)),
            out_shape=(field_shape, field_shape, total_shape),
            in_specs=[anywhere] * 4,
            out_specs=(anywhere, anywhere, inside),
            scratch_shapes=[
                pltpu.VMEM((2, ROWS, ROWS), F32),
                pltpu.VMEM((2, 3, FACE, FACE), F32),
                pltpu.VMEM((2, 2, 5, 64, COLS), F32),
                pltpu.VMEM((2, 2, 5, 64, COLS), F32),
                pltpu.VMEM((2, 384, 384), F32),
                pltpu.VMEM((2, 3, COLS, COLS), F32),
                pltpu.VMEM((2, ROWS, COLS), F32),
                pltpu.VMEM((2, 2, 2 * ROWS, 512), BF16),
                pltpu.VMEM((2, 2 * FACE, COLS), BF16),
                pltpu.VMEM((2, 2, 2 * FACE, COLS), BF16),
                pltpu.VMEM((2, 2 * FACE, 256), BF16),
                pltpu.VMEM((2, 512, 256), BF16),
                pltpu.VMEM((2, COLS, 256), BF16),
                pltpu.VMEM((2, COLS, 256), BF16),
                pltpu.VMEM((2, 256, 256), BF16),
                *[pltpu.VMEM((STEPS, 2, 2, 2, FACE, COLS), F32)] * 4,
                pltpu.VMEM((3, SUMS, COLS), F32),
                pltpu.VMEM((slots, SUMS, COLS), F32),
                pltpu.SemaphoreType.DMA((4,)),
                pltpu.SemaphoreType.DMA((2,)),
                pltpu.SemaphoreType.DMA((STEPS, 2, 2)),
                pltpu.SemaphoreType.DMA((STEPS, 2, 2)),
                pltpu.SemaphoreType.DMA((STEPS, 2, 2, 2)),
                pltpu.SemaphoreType.DMA((STEPS, 2, 2, 2)),
                pltpu.SemaphoreType.DMA((slots + depth - 1,)),
                pltpu.SemaphoreType.DMA((slots,)),
                pltpu.SemaphoreType.REGULAR((TOKENS,)),
            ],
            compiler_params=pltpu.CompilerParams(
                collective_id=0, has_side_effects=True, vmem_limit_bytes=grant
            ),
            name="powers",
        )(
            pin(diagonal.reshape(2, ROWS, ROWS)),
            pin(coupling.reshape(2, 3, FACE, FACE)),
            pin(start_block.reshape(2, 5, 64, COLS)),
            pin(shadow_block.reshape(2, 5, 64, COLS)),
        )
        basis, shadow, moments = pl.pallas_call(
            functools.partial(finish, 1.0 / count),
            out_shape=(field_shape, field_shape, moments_shape),
            in_specs=[anywhere, anywhere, inside],
            out_specs=(anywhere, anywhere, inside),
            scratch_shapes=[pltpu.SemaphoreType.DMA((2, 2))],
            compiler_params=pltpu.CompilerParams(vmem_limit_bytes=grant),
            name="finish",
        )(*powers)
        return basis.reshape(start_block.shape), shadow.reshape(start_block.shape), moments

    placed = P("sub", "dom", None, None, None)
    return jax.shard_map(
        body,
        mesh=mesh,
        in_specs=(placed, P("sub", "dom", None, None, None, None), placed, placed),
        out_specs=(placed, placed, P()),
        check_vma=False,
    )
```

```python
import functools

import jax
import jax.numpy as jnp
from jax import lax
from jax.experimental import pallas as pl
from jax.experimental.pallas import tpu as pltpu
from jax.sharding import PartitionSpec as P

STEPS = 4
ROWS = 320
FACE = 80
COLS = 128
MESH = pl.DeviceIdType.MESH
F32 = jnp.float32
BF16 = jnp.bfloat16
DOWN, UP = range(2)
TOKENS = 6
SUMS = 2 * STEPS + 1


def split(x):
    high = x.astype(BF16)
    return high, (x - high.astype(F32)).astype(BF16)


def put_columns(ref, row, x):
    high, low = split(x)
    rows = pl.ds(row, x.shape[0])
    ref[rows, 0:COLS] = high
    ref[rows, COLS:] = low


def put_rows(ref, row, column, below, x):
    high, low = split(x)
    columns = pl.ds(column, x.shape[1])
    ref[pl.ds(row, x.shape[0]), columns] = high
    ref[pl.ds(row + below, x.shape[0]), columns] = low


def product(left, right):
    full = jnp.dot(left, right, preferred_element_type=F32)
    rows = full.shape[0] // 2
    return full[:rows, :COLS] + (full[:rows, COLS:] + full[rows:, :COLS])


def x_face(ref, node):
    return ref[:, :, node * 16 : node * 16 + 16].reshape(2, FACE, COLS)


def low_half(shape):
    return lax.broadcasted_iota(jnp.int32, shape, len(shape) - 2) < 4


def swap_halves(x):
    return pltpu.roll(x, 4, 1)


def y_parts(u):
    parts = u.reshape(10, 4, 8, COLS)
    return [parts[:, i] for i in range(4)]


def y_low(u):
    first, _, second, _ = y_parts(u)
    return jnp.where(low_half(first.shape), first, swap_halves(second)).reshape(FACE, COLS)


def y_high(u):
    _, first, _, second = y_parts(u)
    return jnp.where(low_half(first.shape), swap_halves(first), second).reshape(FACE, COLS)


def add_y(u, low, high):
    parts = y_parts(u)
    low, high = low.reshape(10, 8, COLS), high.reshape(10, 8, COLS)
    mask = low_half(low.shape)
    zero = jnp.zeros_like(low)
    terms = [
        jnp.where(mask, low, zero),
        jnp.where(mask, zero, swap_halves(high)),
        jnp.where(mask, swap_halves(low), zero),
        jnp.where(mask, zero, high),
    ]
    whole = jnp.concatenate([(part + term)[:, None] for part, term in zip(parts, terms)], axis=1)
    return whole.reshape(5, 64, COLS)


def column_sums(x, y):
    return jnp.sum((x * y).reshape(2 * ROWS, COLS), axis=0, keepdims=True)


def far_first(count):
    return sorted(range(1, count), key=lambda by: -min(by, count - by))


def kernel(
    sizes,
    d_hbm,
    c_hbm,
    b_hbm,
    s_hbm,
    ob_hbm,
    os_hbm,
    total_ref,
    d_in,
    c_in,
    field,
    acc,
    d_pad,
    c_pad,
    z_pad,
    left,
    left_up,
    left_in,
    left_y,
    right,
    right_up,
    right_in,
    right_y,
    x_sent,
    x_got,
    y_sent,
    y_got,
    sums,
    sums_got,
    load_sem,
    store_sem,
    x_send,
    x_recv,
    y_send,
    y_recv,
    sums_send,
    sums_recv,
    token_sem,
):
    doms, subs, depth = sizes
    heights, chips = doms // depth, subs // 2
    dom, sub = lax.axis_index("dom"), lax.axis_index("sub")
    height, level = dom // depth, lax.rem(dom, depth)
    chip, core = sub // 2, lax.rem(sub, 2)

    loads = [
        pltpu.make_async_copy(c_hbm, c_in, load_sem.at[0]),
        pltpu.make_async_copy(b_hbm, field.at[0], load_sem.at[1]),
        pltpu.make_async_copy(s_hbm, field.at[1], load_sem.at[2]),
        pltpu.make_async_copy(d_hbm, d_in, load_sem.at[3]),
    ]
    loads[0].start()
    loads[1].start()

    def on_sub(by):
        return dom, lax.rem(sub + by + subs, subs)

    def on_dom(by):
        return lax.rem(dom + by + doms, doms), sub

    def on_level(by, to=sub):
        return height * depth + lax.rem(level + by + depth, depth), to

    def on_height(by):
        return lax.rem(height + by + heights, heights) * depth + level, sub

    def on_chip(by, to):
        return dom, lax.rem(chip + by, chips) * 2 + to

    near = [on_level(-1), on_level(1), on_height(-1), on_height(1)]
    greeted = [on_dom(-1), on_dom(1), on_sub(-1), on_sub(1)] + near
    barrier = pltpu.get_barrier_semaphore()
    for peer in greeted:
        pl.semaphore_signal(barrier, inc=1, device_id=peer, device_id_type=MESH)

    for load in loads[2:]:
        load.start()

    def pass_token(step):
        for peer in near:
            pl.semaphore_signal(token_sem.at[step], inc=1, device_id=peer, device_id_type=MESH)

    def x_message(k, f, way):
        return pltpu.make_async_remote_copy(
            src_ref=x_sent.at[k, f, way],
            dst_ref=x_got.at[k, f, way],
            send_sem=x_send.at[k, f, way],
            recv_sem=x_recv.at[k, f, way],
            device_id=on_sub(2 * way - 1),
            device_id_type=MESH,
        )

    def y_message(k, f, way, e):
        return pltpu.make_async_remote_copy(
            src_ref=y_sent.at[k, f, way, e],
            dst_ref=y_got.at[k, f, way, e],
            send_sem=y_send.at[k, f, way, e],
            recv_sem=y_recv.at[k, f, way, e],
            device_id=on_dom(2 * way - 1),
            device_id_type=MESH,
        )

    def through(lefts, e, rights, x):
        put_columns(rights.at[e], 0, x)
        return product(lefts[e], rights[e])

    def y_down(k, f, e, trace):
        y_sent[k, f, DOWN, e] = trace
        y_message(k, f, DOWN, e).start()

    def y_up(k, f, e):
        y_sent[k, f, UP, e] = product(left_y[e], right_y[e])
        y_message(k, f, UP, e).start()

    def x_down(k, f):
        x_sent[k, f, DOWN] = x_face(field.at[f], 0)
        x_message(k, f, DOWN).start()

    def x_up(k, f):
        trace = x_face(field.at[f], 3)
        for e in range(2):
            x_sent[k, f, UP, e] = through(left_up, e, right_up, trace[e])
        x_message(k, f, UP).start()

    for ref in (c_pad, right_up, right_in, left_y, right_y):
        ref[...] = jnp.zeros_like(ref)

    loads[0].wait()
    for e in range(2):
        for side, last in enumerate((sub == subs - 1, dom == doms - 1)):
            c_pad[e, side, 0:FACE, 0:FACE] = jnp.where(last, 0.0, c_in[e, side])
        c_pad[e, 2, 0:FACE, 0:FACE] = c_in[e, 2]
    for e in range(2):
        put_rows(left_y.at[e], 0, 0, FACE, c_pad[e, 1].T[:FACE])
        put_rows(left_up.at[e], 0, 0, FACE, c_pad[e, 0].T[:FACE])

    def first_traces(f):
        loads[1 + f].wait()
        for e in range(2):
            y_sent[0, f, DOWN, e] = y_low(field[f, e])
            put_columns(right_y.at[e], 0, y_high(field[f, e]))
            y_sent[0, f, UP, e] = product(left_y[e], right_y[e])
        x_sent[0, f, DOWN] = x_face(field.at[f], 0)
        trace = x_face(field.at[f], 3)
        for e in range(2):
            x_sent[0, f, UP, e] = through(left_up, e, right_up, trace[e])

    def first_sends(f):
        for e in range(2):
            for way in range(2):
                y_message(0, f, way, e).start()
        for way in range(2):
            x_message(0, f, way).start()

    first_traces(0)
    first_traces(1)
    pl.semaphore_wait(barrier, len(greeted))
    first_sends(0)
    first_sends(1)
    pass_token(0)

    for side in range(2):
        for e in range(2):
            put_rows(left_in.at[side, e], 0, 0, FACE, c_pad[e, side, 0:FACE])
    for e in range(2):
        put_columns(right_in.at[e], 0, c_pad[e, 1, 0:FACE])
        put_rows(left_y.at[e], 0, COLS, FACE, product(left_y[e, :, 0:COLS], right_in[e]))
    for ref in (z_pad, d_pad, left, right):
        ref[...] = jnp.zeros_like(ref)
    z_pad[0, pl.ds(3, FACE, stride=4), :] = c_pad[0, 2, 0:FACE]
    z_pad[1, pl.ds(0, FACE, stride=4), :] = -c_pad[0, 2].T[:FACE]
    loads[3].wait()
    for e in range(2):
        d_pad[e, 0:ROWS, 0:ROWS] = d_in[e]
        put_rows(left.at[0, e], 0, 0, ROWS, d_pad[e, 0:ROWS, :])
        put_rows(left.at[0, e], 0, 384, ROWS, z_pad[e])
        put_rows(left.at[1, e], 0, 384, ROWS, -z_pad[e])
        for i in range(3):
            rows = min(COLS, ROWS - i * COLS)
            for j in range(3):
                block = d_pad[e, j * COLS : (j + 1) * COLS, i * COLS : (i + 1) * COLS].T
                put_rows(left.at[1, e], i * COLS, j * COLS, ROWS, block[:rows])

    def local_part(f):
        flat = field.at[f].reshape(2, ROWS, COLS)
        for e in range(2):
            put_columns(right.at[e], 0, flat[e])
            put_columns(right.at[e], 384, flat[1 - e, pl.ds(3 * e, FACE, stride=4), :])
        for e in range(2):
            acc[f, e] = product(left[f, e], right[e]).reshape(5, 64, COLS)

    for f in range(2):
        local_part(f)
    sums[0, 0:1] = column_sums(field[1], field[0])

    for k in range(STEPS):
        more = k + 1 < STEPS
        for f in range(2):
            sign = 1.0 - 2.0 * f
            for way in (UP, DOWN):
                x_message(k, f, way).wait_recv()
            for e in range(2):
                into = through(left_in.at[0], e, right_in, x_got[k, f, DOWN, e]).reshape(5, 16, COLS)
                acc[f, e, :, 48:64] = acc[f, e, :, 48:64] + sign * into
                back = x_got[k, f, UP, e].reshape(5, 16, COLS)
                acc[f, e, :, 0:16] = acc[f, e, :, 0:16] - sign * back
            if more:
                for e in range(2):
                    put_columns(right_y.at[e], 0, y_high(acc[f, e]))

            def from_above(e):
                y_message(k, f, DOWN, e).wait_recv()
                put_columns(right_y.at[e], COLS, sign * y_got[k, f, DOWN, e])
                if more:
                    y_up(k + 1, f, e)

            def from_below(e):
                y_message(k, f, UP, e).wait_recv()
                if more:
                    y_down(k + 1, f, e, y_low(acc[f, e]) - sign * y_got[k, f, UP, e])

            for e in range(2):
                from_below(e)
                from_above(e)
            for e in range(2):
                high = product(left_in[1, e], right_y[e, COLS:])
                field[f, e] = add_y(acc[f, e], -sign * y_got[k, f, UP, e], high)
            if more:
                x_down(k + 1, f)
                x_up(k + 1, f)
            else:
                pltpu.make_async_copy(field.at[f], (ob_hbm, os_hbm)[f], store_sem.at[f]).start()
            moment = 2 * k + 1 + f
            sums[0, moment : moment + 1] = column_sums(field[1], field[0])
            step = 2 * k + f
            if step < TOKENS:
                pl.semaphore_wait(token_sem.at[step], len(near))
                if step + 1 < TOKENS:
                    pass_token(step + 1)
            if more and f == 1:
                local_part(0)
                local_part(1)

    def total_copy(stage, slot, peer, send=None):
        return pltpu.make_async_remote_copy(
            src_ref=sums.at[stage],
            dst_ref=sums_got.at[slot],
            send_sem=sums_send.at[slot if send is None else send],
            recv_sem=sums_recv.at[slot],
            device_id=peer,
            device_id_type=MESH,
        )

    def arrived(total, stage, first, count):
        for slot in range(first, first + count):
            total_copy(stage, slot, on_level(1)).wait_recv()
            total = total + sums_got[slot]
        return total

    inner, outer = on_chip(0, 0), on_chip(0, 1)
    across = far_first(chips)
    slot_in, slot_y = 2 * len(across), 2 * len(across) + 1
    slot_z = slot_y + heights - 1
    slot_out = slot_z + depth - 1

    def settle():
        for k in range(STEPS):
            for f in range(2):
                for way in range(2):
                    x_message(k, f, way).wait_send()
                    for e in range(2):
                        y_message(k, f, way, e).wait_send()
        for f in range(2):
            pltpu.make_async_copy(field.at[f], (ob_hbm, os_hbm)[f], store_sem.at[f]).wait()

    @pl.when(core == 0)
    def _():
        copies = [total_copy(0, i, on_chip(by, 1)) for i, by in enumerate(across)]
        copies.append(total_copy(0, slot_in, outer))
        for copy in copies:
            copy.start()
        settle()
        for copy in copies:
            copy.wait_send()
        total_copy(2, slot_out, outer).wait_recv()
        total_ref[...] = arrived(sums_got[slot_out], 2, slot_z, depth - 1)

    @pl.when(core == 1)
    def _():
        copies = [total_copy(0, len(across) + i, on_chip(by, 1)) for i, by in enumerate(across)]
        for copy in copies:
            copy.start()
        settle()
        for copy in copies:
            copy.wait_send()
        sums[1] = arrived(sums[0], 0, 0, slot_y)
        along_y = [total_copy(1, slot_y + i, on_height(by)) for i, by in enumerate(far_first(heights))]
        for copy in along_y:
            copy.start()
        for copy in along_y:
            copy.wait_send()
        sums[2] = arrived(sums[1], 1, slot_y, heights - 1)
        along_z = []
        for i in range(depth - 1):
            after = (i + depth - level) // depth
            place = height * depth + i + after
            slot = slot_z + level - 1 + after
            along_z.append(total_copy(2, slot, (place, chip * 2), slot_z + i))
            along_z.append(total_copy(2, slot, (place, sub), slot_out + 1 + i))
        along_z.append(total_copy(2, slot_out, inner))
        for copy in along_z:
            copy.start()
        for copy in along_z:
            copy.wait_send()
        total_ref[...] = arrived(sums[2], 2, slot_z, depth - 1)


def pin(x):
    return pltpu.with_memory_space_constraint(x, pltpu.HBM)


def finish(scale, b_hbm, s_hbm, total_ref, ob_hbm, os_hbm, moments_hbm, moments_ref, moments_sem, sem):
    copies = [
        pltpu.make_async_copy(b_hbm.at[e], ob_hbm.at[e], sem.at[0, e]) for e in range(2)
    ] + [pltpu.make_async_copy(s_hbm.at[e], os_hbm.at[e], sem.at[1, e]) for e in range(2)]
    for copy in copies:
        copy.start()
    total = total_ref[...] * scale
    for i in range(STEPS + 1):
        moments_ref[i] = total[i : i + STEPS + 1]
    copies.append(pltpu.make_async_copy(moments_ref, moments_hbm, moments_sem))
    copies[-1].start()
    for copy in copies:
        copy.wait()


def solution(mesh):
    doms, subs = mesh.shape["dom"], mesh.shape["sub"]
    depth = 12
    slots = 2 * (subs // 2 - 1) + 1 + (doms // depth - 1) + (depth - 1) + 1
    anywhere = pl.BlockSpec(memory_space=pl.ANY)
    inside = pl.BlockSpec(memory_space=pltpu.VMEM)
    grant = 40 * 1024 * 1024

    def body(diagonal, coupling, start_block, shadow_block):
        count = 2 * ROWS * doms * subs
        field_shape = jax.ShapeDtypeStruct((2, 5, 64, COLS), F32)
        moments_shape = jax.ShapeDtypeStruct((STEPS + 1, STEPS + 1, COLS), F32)
        total_shape = jax.ShapeDtypeStruct((SUMS, COLS), F32)
        powers = pl.pallas_call(
            functools.partial(kernel, (doms, subs, depth)),
            out_shape=(field_shape, field_shape, total_shape),
            in_specs=[anywhere] * 4,
            out_specs=(anywhere, anywhere, inside),
            scratch_shapes=[
                pltpu.VMEM((2, ROWS, ROWS), F32),
                pltpu.VMEM((2, 3, FACE, FACE), F32),
                pltpu.VMEM((2, 2, 5, 64, COLS), F32),
                pltpu.VMEM((2, 2, 5, 64, COLS), F32),
                pltpu.VMEM((2, 384, 384), F32),
                pltpu.VMEM((2, 3, COLS, COLS), F32),
                pltpu.VMEM((2, ROWS, COLS), F32),
                pltpu.VMEM((2, 2, 2 * ROWS, 512), BF16),
                pltpu.VMEM((2, 2 * FACE, COLS), BF16),
                pltpu.VMEM((2, 2, 2 * FACE, COLS), BF16),
                pltpu.VMEM((2, 2 * FACE, 256), BF16),
                pltpu.VMEM((2, 512, 256), BF16),
                pltpu.VMEM((2, COLS, 256), BF16),
                pltpu.VMEM((2, COLS, 256), BF16),
                pltpu.VMEM((2, 256, 256), BF16),
                *[pltpu.VMEM((STEPS, 2, 2, 2, FACE, COLS), F32)] * 4,
                pltpu.VMEM((3, SUMS, COLS), F32),
                pltpu.VMEM((slots, SUMS, COLS), F32),
                pltpu.SemaphoreType.DMA((4,)),
                pltpu.SemaphoreType.DMA((2,)),
                pltpu.SemaphoreType.DMA((STEPS, 2, 2)),
                pltpu.SemaphoreType.DMA((STEPS, 2, 2)),
                pltpu.SemaphoreType.DMA((STEPS, 2, 2, 2)),
                pltpu.SemaphoreType.DMA((STEPS, 2, 2, 2)),
                pltpu.SemaphoreType.DMA((slots + depth - 1,)),
                pltpu.SemaphoreType.DMA((slots,)),
                pltpu.SemaphoreType.REGULAR((TOKENS,)),
            ],
            compiler_params=pltpu.CompilerParams(
                collective_id=0, has_side_effects=True, vmem_limit_bytes=grant
            ),
            name="powers",
        )(
            pin(diagonal.reshape(2, ROWS, ROWS)),
            pin(coupling.reshape(2, 3, FACE, FACE)),
            pin(start_block.reshape(2, 5, 64, COLS)),
            pin(shadow_block.reshape(2, 5, 64, COLS)),
        )
        basis, shadow, moments = pl.pallas_call(
            functools.partial(finish, 1.0 / count),
            out_shape=(field_shape, field_shape, moments_shape),
            in_specs=[anywhere, anywhere, inside],
            out_specs=(anywhere, anywhere, anywhere),
            scratch_shapes=[pltpu.VMEM((STEPS + 1, STEPS + 1, COLS), F32), pltpu.SemaphoreType.DMA, pltpu.SemaphoreType.DMA((2, 2))],
            compiler_params=pltpu.CompilerParams(vmem_limit_bytes=grant),
            name="finish",
        )(*powers)
        return basis.reshape(start_block.shape), shadow.reshape(start_block.shape), moments

    placed = P("sub", "dom", None, None, None)
    return jax.shard_map(
        body,
        mesh=mesh,
        in_specs=(placed, P("sub", "dom", None, None, None, None), placed, placed),
        out_specs=(placed, placed, P()),
        check_vma=False,
    )
```

```python
import functools

import jax
import jax.numpy as jnp
from jax import lax
from jax.experimental import pallas as pl
from jax.experimental.pallas import tpu as pltpu
from jax.sharding import PartitionSpec as P

STEPS = 4
ROWS = 320
FACE = 80
COLS = 128
MESH = pl.DeviceIdType.MESH
F32 = jnp.float32
BF16 = jnp.bfloat16
DOWN, UP = range(2)
TOKENS = 6
SUMS = 2 * STEPS + 1


def split(x):
    high = x.astype(BF16)
    return high, (x - high.astype(F32)).astype(BF16)


def put_columns(ref, row, x):
    high, low = split(x)
    rows = pl.ds(row, x.shape[0])
    ref[rows, 0:COLS] = high
    ref[rows, COLS:] = low


def put_rows(ref, row, column, below, x):
    high, low = split(x)
    columns = pl.ds(column, x.shape[1])
    ref[pl.ds(row, x.shape[0]), columns] = high
    ref[pl.ds(row + below, x.shape[0]), columns] = low


def product(left, right):
    full = jnp.dot(left, right, preferred_element_type=F32)
    rows = full.shape[0] // 2
    return full[:rows, :COLS] + (full[:rows, COLS:] + full[rows:, :COLS])


def x_face(ref, node):
    return ref[:, :, node * 16 : node * 16 + 16].reshape(2, FACE, COLS)


def low_half(shape):
    return lax.broadcasted_iota(jnp.int32, shape, len(shape) - 2) < 4


def swap_halves(x):
    return pltpu.roll(x, 4, 1)


def y_parts(u):
    parts = u.reshape(10, 4, 8, COLS)
    return [parts[:, i] for i in range(4)]


def y_low(u):
    first, _, second, _ = y_parts(u)
    return jnp.where(low_half(first.shape), first, swap_halves(second)).reshape(FACE, COLS)


def y_high(u):
    _, first, _, second = y_parts(u)
    return jnp.where(low_half(first.shape), swap_halves(first), second).reshape(FACE, COLS)


def add_y(u, low, high):
    parts = y_parts(u)
    low, high = low.reshape(10, 8, COLS), high.reshape(10, 8, COLS)
    mask = low_half(low.shape)
    zero = jnp.zeros_like(low)
    terms = [
        jnp.where(mask, low, zero),
        jnp.where(mask, zero, swap_halves(high)),
        jnp.where(mask, swap_halves(low), zero),
        jnp.where(mask, zero, high),
    ]
    whole = jnp.concatenate([(part + term)[:, None] for part, term in zip(parts, terms)], axis=1)
    return whole.reshape(5, 64, COLS)


def column_sums(x, y):
    return jnp.sum((x * y).reshape(-1, COLS), axis=0, keepdims=True)


def far_first(count):
    return sorted(range(1, count), key=lambda by: -min(by, count - by))


def kernel(
    sizes,
    d_hbm,
    c_hbm,
    b_hbm,
    s_hbm,
    ob_hbm,
    os_hbm,
    total_ref,
    d_in,
    c_in,
    field,
    acc,
    d_pad,
    c_pad,
    z_pad,
    left,
    left_up,
    left_in,
    left_y,
    right,
    right_up,
    right_in,
    right_y,
    x_sent,
    x_got,
    y_sent,
    y_got,
    sums,
    sums_got,
    load_sem,
    store_sem,
    x_send,
    x_recv,
    y_send,
    y_recv,
    sums_send,
    sums_recv,
    token_sem,
):
    doms, subs, depth = sizes
    heights, chips = doms // depth, subs // 2
    dom, sub = lax.axis_index("dom"), lax.axis_index("sub")
    height, level = dom // depth, lax.rem(dom, depth)
    chip, core = sub // 2, lax.rem(sub, 2)

    loads = [
        pltpu.make_async_copy(c_hbm, c_in, load_sem.at[0]),
        pltpu.make_async_copy(b_hbm, field.at[0], load_sem.at[1]),
        pltpu.make_async_copy(s_hbm, field.at[1], load_sem.at[2]),
        pltpu.make_async_copy(d_hbm, d_in, load_sem.at[3]),
    ]
    loads[0].start()
    loads[1].start()

    def on_sub(by):
        return dom, lax.rem(sub + by + subs, subs)

    def on_dom(by):
        return lax.rem(dom + by + doms, doms), sub

    def on_level(by, to=sub):
        return height * depth + lax.rem(level + by + depth, depth), to

    def on_height(by):
        return lax.rem(height + by + heights, heights) * depth + level, sub

    def on_chip(by, to):
        return dom, lax.rem(chip + by, chips) * 2 + to

    near = [on_level(-1), on_level(1), on_height(-1), on_height(1)]
    greeted = [on_dom(-1), on_dom(1), on_sub(-1), on_sub(1)] + near
    barrier = pltpu.get_barrier_semaphore()
    for peer in greeted:
        pl.semaphore_signal(barrier, inc=1, device_id=peer, device_id_type=MESH)

    for load in loads[2:]:
        load.start()

    def pass_token(step):
        for peer in near:
            pl.semaphore_signal(token_sem.at[step], inc=1, device_id=peer, device_id_type=MESH)

    def x_message(k, f, way):
        return pltpu.make_async_remote_copy(
            src_ref=x_sent.at[k, f, way],
            dst_ref=x_got.at[k, f, way],
            send_sem=x_send.at[k, f, way],
            recv_sem=x_recv.at[k, f, way],
            device_id=on_sub(2 * way - 1),
            device_id_type=MESH,
        )

    def y_message(k, f, way, e):
        return pltpu.make_async_remote_copy(
            src_ref=y_sent.at[k, f, way, e],
            dst_ref=y_got.at[k, f, way, e],
            send_sem=y_send.at[k, f, way, e],
            recv_sem=y_recv.at[k, f, way, e],
            device_id=on_dom(2 * way - 1),
            device_id_type=MESH,
        )

    def through(lefts, e, rights, x):
        put_columns(rights.at[e], 0, x)
        return product(lefts[e], rights[e])

    def y_down(k, f, e, trace):
        y_sent[k, f, DOWN, e] = trace
        y_message(k, f, DOWN, e).start()

    def y_up(k, f, e):
        y_sent[k, f, UP, e] = product(left_y[e], right_y[e])
        y_message(k, f, UP, e).start()

    def x_down(k, f):
        x_sent[k, f, DOWN] = x_face(field.at[f], 0)
        x_message(k, f, DOWN).start()

    def x_up(k, f):
        trace = x_face(field.at[f], 3)
        for e in range(2):
            x_sent[k, f, UP, e] = through(left_up, e, right_up, trace[e])
        x_message(k, f, UP).start()

    for ref in (c_pad, right_up, right_in, left_y, right_y):
        ref[...] = jnp.zeros_like(ref)

    loads[0].wait()
    for e in range(2):
        for side, last in enumerate((sub == subs - 1, dom == doms - 1)):
            c_pad[e, side, 0:FACE, 0:FACE] = jnp.where(last, 0.0, c_in[e, side])
        c_pad[e, 2, 0:FACE, 0:FACE] = c_in[e, 2]
    for e in range(2):
        put_rows(left_y.at[e], 0, 0, FACE, c_pad[e, 1].T[:FACE])
        put_rows(left_up.at[e], 0, 0, FACE, c_pad[e, 0].T[:FACE])

    def first_traces(f):
        loads[1 + f].wait()
        for e in range(2):
            y_sent[0, f, DOWN, e] = y_low(field[f, e])
            put_columns(right_y.at[e], 0, y_high(field[f, e]))
            y_sent[0, f, UP, e] = product(left_y[e], right_y[e])
        x_sent[0, f, DOWN] = x_face(field.at[f], 0)
        trace = x_face(field.at[f], 3)
        for e in range(2):
            x_sent[0, f, UP, e] = through(left_up, e, right_up, trace[e])

    def first_sends(f):
        for e in range(2):
            for way in range(2):
                y_message(0, f, way, e).start()
        for way in range(2):
            x_message(0, f, way).start()

    first_traces(0)
    first_traces(1)
    pl.semaphore_wait(barrier, len(greeted))
    first_sends(0)
    first_sends(1)
    pass_token(0)

    for side in range(2):
        for e in range(2):
            put_rows(left_in.at[side, e], 0, 0, FACE, c_pad[e, side, 0:FACE])
    for e in range(2):
        put_columns(right_in.at[e], 0, c_pad[e, 1, 0:FACE])
        put_rows(left_y.at[e], 0, COLS, FACE, product(left_y[e, :, 0:COLS], right_in[e]))
    for ref in (z_pad, d_pad, left, right):
        ref[...] = jnp.zeros_like(ref)
    z_pad[0, pl.ds(3, FACE, stride=4), :] = c_pad[0, 2, 0:FACE]
    z_pad[1, pl.ds(0, FACE, stride=4), :] = -c_pad[0, 2].T[:FACE]
    loads[3].wait()
    for e in range(2):
        d_pad[e, 0:ROWS, 0:ROWS] = d_in[e]
        put_rows(left.at[0, e], 0, 0, ROWS, d_pad[e, 0:ROWS, :])
        put_rows(left.at[0, e], 0, 384, ROWS, z_pad[e])
        put_rows(left.at[1, e], 0, 384, ROWS, -z_pad[e])
        for i in range(3):
            rows = min(COLS, ROWS - i * COLS)
            for j in range(3):
                block = d_pad[e, j * COLS : (j + 1) * COLS, i * COLS : (i + 1) * COLS].T
                put_rows(left.at[1, e], i * COLS, j * COLS, ROWS, block[:rows])

    def local_part(f):
        flat = field.at[f].reshape(2, ROWS, COLS)
        for e in range(2):
            put_columns(right.at[e], 0, flat[e])
            put_columns(right.at[e], 384, flat[1 - e, pl.ds(3 * e, FACE, stride=4), :])
        for e in range(2):
            acc[f, e] = product(left[f, e], right[e]).reshape(5, 64, COLS)

    for f in range(2):
        local_part(f)
    sums[0, 0:1] = column_sums(field[1], field[0])

    for k in range(STEPS):
        more = k + 1 < STEPS
        for f in range(2):
            sign = 1.0 - 2.0 * f
            for way in (UP, DOWN):
                x_message(k, f, way).wait_recv()
            for e in range(2):
                into = through(left_in.at[0], e, right_in, x_got[k, f, DOWN, e]).reshape(5, 16, COLS)
                acc[f, e, :, 48:64] = acc[f, e, :, 48:64] + sign * into
                back = x_got[k, f, UP, e].reshape(5, 16, COLS)
                acc[f, e, :, 0:16] = acc[f, e, :, 0:16] - sign * back
            if more:
                for e in range(2):
                    put_columns(right_y.at[e], 0, y_high(acc[f, e]))

            def from_above(e):
                y_message(k, f, DOWN, e).wait_recv()
                put_columns(right_y.at[e], COLS, sign * y_got[k, f, DOWN, e])
                if more:
                    y_up(k + 1, f, e)

            def from_below(e):
                y_message(k, f, UP, e).wait_recv()
                if more:
                    y_down(k + 1, f, e, y_low(acc[f, e]) - sign * y_got[k, f, UP, e])

            def update(e):
                high = product(left_in[1, e], right_y[e, COLS:])
                field[f, e] = add_y(acc[f, e], -sign * y_got[k, f, UP, e], high)
                return column_sums(field[1, e], field[0, e])

            parts = []
            for e in range(2):
                from_below(e)
                from_above(e)
                parts.append(update(e))
            if more:
                x_down(k + 1, f)
                x_up(k + 1, f)
            else:
                pltpu.make_async_copy(field.at[f], (ob_hbm, os_hbm)[f], store_sem.at[f]).start()
            moment = 2 * k + 1 + f
            sums[0, moment : moment + 1] = parts[0] + parts[1]
            step = 2 * k + f
            if step < TOKENS:
                pl.semaphore_wait(token_sem.at[step], len(near))
                if step + 1 < TOKENS:
                    pass_token(step + 1)
            if more and f == 1:
                local_part(0)
                local_part(1)

    def total_copy(stage, slot, peer, send=None):
        return pltpu.make_async_remote_copy(
            src_ref=sums.at[stage],
            dst_ref=sums_got.at[slot],
            send_sem=sums_send.at[slot if send is None else send],
            recv_sem=sums_recv.at[slot],
            device_id=peer,
            device_id_type=MESH,
        )

    def arrived(total, stage, first, count):
        for slot in range(first, first + count):
            total_copy(stage, slot, on_level(1)).wait_recv()
            total = total + sums_got[slot]
        return total

    inner, outer = on_chip(0, 0), on_chip(0, 1)
    across = far_first(chips)
    slot_in, slot_y = 2 * len(across), 2 * len(across) + 1
    slot_z = slot_y + heights - 1
    slot_out = slot_z + depth - 1

    def settle():
        for k in range(STEPS):
            for f in range(2):
                for way in range(2):
                    x_message(k, f, way).wait_send()
                    for e in range(2):
                        y_message(k, f, way, e).wait_send()
        for f in range(2):
            pltpu.make_async_copy(field.at[f], (ob_hbm, os_hbm)[f], store_sem.at[f]).wait()

    @pl.when(core == 0)
    def _():
        copies = [total_copy(0, i, on_chip(by, 1)) for i, by in enumerate(across)]
        copies.append(total_copy(0, slot_in, outer))
        for copy in copies:
            copy.start()
        settle()
        for copy in copies:
            copy.wait_send()
        total_copy(2, slot_out, outer).wait_recv()
        total_ref[...] = arrived(sums_got[slot_out], 2, slot_z, depth - 1)

    @pl.when(core == 1)
    def _():
        copies = [total_copy(0, len(across) + i, on_chip(by, 1)) for i, by in enumerate(across)]
        for copy in copies:
            copy.start()
        settle()
        for copy in copies:
            copy.wait_send()
        sums[1] = arrived(sums[0], 0, 0, slot_y)
        along_y = [total_copy(1, slot_y + i, on_height(by)) for i, by in enumerate(far_first(heights))]
        for copy in along_y:
            copy.start()
        for copy in along_y:
            copy.wait_send()
        sums[2] = arrived(sums[1], 1, slot_y, heights - 1)
        along_z = []
        for i in range(depth - 1):
            after = (i + depth - level) // depth
            place = height * depth + i + after
            slot = slot_z + level - 1 + after
            along_z.append(total_copy(2, slot, (place, chip * 2), slot_z + i))
            along_z.append(total_copy(2, slot, (place, sub), slot_out + 1 + i))
        along_z.append(total_copy(2, slot_out, inner))
        for copy in along_z:
            copy.start()
        for copy in along_z:
            copy.wait_send()
        total_ref[...] = arrived(sums[2], 2, slot_z, depth - 1)


def pin(x):
    return pltpu.with_memory_space_constraint(x, pltpu.HBM)


def finish(scale, b_hbm, s_hbm, total_ref, ob_hbm, os_hbm, moments_hbm, moments_ref, moments_sem, sem):
    copies = [
        pltpu.make_async_copy(b_hbm.at[e], ob_hbm.at[e], sem.at[0, e]) for e in range(2)
    ] + [pltpu.make_async_copy(s_hbm.at[e], os_hbm.at[e], sem.at[1, e]) for e in range(2)]
    for copy in copies:
        copy.start()
    total = total_ref[...] * scale
    for i in range(STEPS + 1):
        moments_ref[i] = total[i : i + STEPS + 1]
    copies.append(pltpu.make_async_copy(moments_ref, moments_hbm, moments_sem))
    copies[-1].start()
    for copy in copies:
        copy.wait()


def solution(mesh):
    doms, subs = mesh.shape["dom"], mesh.shape["sub"]
    depth = 12
    slots = 2 * (subs // 2 - 1) + 1 + (doms // depth - 1) + (depth - 1) + 1
    anywhere = pl.BlockSpec(memory_space=pl.ANY)
    inside = pl.BlockSpec(memory_space=pltpu.VMEM)
    grant = 40 * 1024 * 1024

    def body(diagonal, coupling, start_block, shadow_block):
        count = 2 * ROWS * doms * subs
        field_shape = jax.ShapeDtypeStruct((2, 5, 64, COLS), F32)
        moments_shape = jax.ShapeDtypeStruct((STEPS + 1, STEPS + 1, COLS), F32)
        total_shape = jax.ShapeDtypeStruct((SUMS, COLS), F32)
        powers = pl.pallas_call(
            functools.partial(kernel, (doms, subs, depth)),
            out_shape=(field_shape, field_shape, total_shape),
            in_specs=[anywhere] * 4,
            out_specs=(anywhere, anywhere, inside),
            scratch_shapes=[
                pltpu.VMEM((2, ROWS, ROWS), F32),
                pltpu.VMEM((2, 3, FACE, FACE), F32),
                pltpu.VMEM((2, 2, 5, 64, COLS), F32),
                pltpu.VMEM((2, 2, 5, 64, COLS), F32),
                pltpu.VMEM((2, 384, 384), F32),
                pltpu.VMEM((2, 3, COLS, COLS), F32),
                pltpu.VMEM((2, ROWS, COLS), F32),
                pltpu.VMEM((2, 2, 2 * ROWS, 512), BF16),
                pltpu.VMEM((2, 2 * FACE, COLS), BF16),
                pltpu.VMEM((2, 2, 2 * FACE, COLS), BF16),
                pltpu.VMEM((2, 2 * FACE, 256), BF16),
                pltpu.VMEM((2, 512, 256), BF16),
                pltpu.VMEM((2, COLS, 256), BF16),
                pltpu.VMEM((2, COLS, 256), BF16),
                pltpu.VMEM((2, 256, 256), BF16),
                *[pltpu.VMEM((STEPS, 2, 2, 2, FACE, COLS), F32)] * 4,
                pltpu.VMEM((3, SUMS, COLS), F32),
                pltpu.VMEM((slots, SUMS, COLS), F32),
                pltpu.SemaphoreType.DMA((4,)),
                pltpu.SemaphoreType.DMA((2,)),
                pltpu.SemaphoreType.DMA((STEPS, 2, 2)),
                pltpu.SemaphoreType.DMA((STEPS, 2, 2)),
                pltpu.SemaphoreType.DMA((STEPS, 2, 2, 2)),
                pltpu.SemaphoreType.DMA((STEPS, 2, 2, 2)),
                pltpu.SemaphoreType.DMA((slots + depth - 1,)),
                pltpu.SemaphoreType.DMA((slots,)),
                pltpu.SemaphoreType.REGULAR((TOKENS,)),
            ],
            compiler_params=pltpu.CompilerParams(
                collective_id=0, has_side_effects=True, vmem_limit_bytes=grant
            ),
            name="powers",
        )(
            pin(diagonal.reshape(2, ROWS, ROWS)),
            pin(coupling.reshape(2, 3, FACE, FACE)),
            pin(start_block.reshape(2, 5, 64, COLS)),
            pin(shadow_block.reshape(2, 5, 64, COLS)),
        )
        basis, shadow, moments = pl.pallas_call(
            functools.partial(finish, 1.0 / count),
            out_shape=(field_shape, field_shape, moments_shape),
            in_specs=[anywhere, anywhere, inside],
            out_specs=(anywhere, anywhere, anywhere),
            scratch_shapes=[pltpu.VMEM((STEPS + 1, STEPS + 1, COLS), F32), pltpu.SemaphoreType.DMA, pltpu.SemaphoreType.DMA((2, 2))],
            compiler_params=pltpu.CompilerParams(vmem_limit_bytes=grant),
            name="finish",
        )(*powers)
        return basis.reshape(start_block.shape), shadow.reshape(start_block.shape), moments

    placed = P("sub", "dom", None, None, None)
    return jax.shard_map(
        body,
        mesh=mesh,
        in_specs=(placed, P("sub", "dom", None, None, None, None), placed, placed),
        out_specs=(placed, placed, P()),
        check_vma=False,
    )
```

```python
import functools

import jax
import jax.numpy as jnp
from jax import lax
from jax.experimental import pallas as pl
from jax.experimental.pallas import tpu as pltpu
from jax.sharding import PartitionSpec as P

STEPS = 4
ROWS = 320
FACE = 80
COLS = 128
MESH = pl.DeviceIdType.MESH
F32 = jnp.float32
BF16 = jnp.bfloat16
DOWN, UP = range(2)
TOKENS = 6
SUMS = 2 * STEPS + 1


def split(x):
    high = x.astype(BF16)
    return high, (x - high.astype(F32)).astype(BF16)


def put_columns(ref, row, x):
    high, low = split(x)
    rows = pl.ds(row, x.shape[0])
    ref[rows, 0:COLS] = high
    ref[rows, COLS:] = low


def put_rows(ref, row, column, below, x):
    high, low = split(x)
    columns = pl.ds(column, x.shape[1])
    ref[pl.ds(row, x.shape[0]), columns] = high
    ref[pl.ds(row + below, x.shape[0]), columns] = low


def product(left, right):
    full = jnp.dot(left, right, preferred_element_type=F32)
    rows = full.shape[0] // 2
    return full[:rows, :COLS] + (full[:rows, COLS:] + full[rows:, :COLS])


def x_face(ref, node):
    return ref[:, :, node * 16 : node * 16 + 16].reshape(2, FACE, COLS)


def low_half(shape):
    return lax.broadcasted_iota(jnp.int32, shape, len(shape) - 2) < 4


def swap_halves(x):
    return pltpu.roll(x, 4, 1)


def y_parts(u):
    parts = u.reshape(10, 4, 8, COLS)
    return [parts[:, i] for i in range(4)]


def y_low(u):
    first, _, second, _ = y_parts(u)
    return jnp.where(low_half(first.shape), first, swap_halves(second)).reshape(FACE, COLS)


def y_high(u):
    _, first, _, second = y_parts(u)
    return jnp.where(low_half(first.shape), swap_halves(first), second).reshape(FACE, COLS)


def add_y(u, low, high):
    parts = y_parts(u)
    low, high = low.reshape(10, 8, COLS), high.reshape(10, 8, COLS)
    mask = low_half(low.shape)
    zero = jnp.zeros_like(low)
    terms = [
        jnp.where(mask, low, zero),
        jnp.where(mask, zero, swap_halves(high)),
        jnp.where(mask, swap_halves(low), zero),
        jnp.where(mask, zero, high),
    ]
    whole = jnp.concatenate([(part + term)[:, None] for part, term in zip(parts, terms)], axis=1)
    return whole.reshape(5, 64, COLS)


def column_sums(x, y):
    return jnp.sum((x * y).reshape(-1, COLS), axis=0, keepdims=True)


def far_first(count):
    return sorted(range(1, count), key=lambda by: -min(by, count - by))


def kernel(
    sizes,
    d_hbm,
    c_hbm,
    b_hbm,
    s_hbm,
    ob_hbm,
    os_hbm,
    total_ref,
    d_in,
    c_in,
    field,
    acc,
    d_pad,
    c_pad,
    z_pad,
    left,
    left_up,
    left_in,
    left_y,
    right,
    right_up,
    right_in,
    right_y,
    x_sent,
    x_got,
    y_sent,
    y_got,
    sums,
    sums_got,
    load_sem,
    store_sem,
    x_send,
    x_recv,
    y_send,
    y_recv,
    sums_send,
    sums_recv,
    token_sem,
):
    doms, subs, depth = sizes
    heights, chips = doms // depth, subs // 2
    dom, sub = lax.axis_index("dom"), lax.axis_index("sub")
    height, level = dom // depth, lax.rem(dom, depth)
    chip, core = sub // 2, lax.rem(sub, 2)

    loads = [
        pltpu.make_async_copy(c_hbm, c_in, load_sem.at[0]),
        pltpu.make_async_copy(b_hbm, field.at[0], load_sem.at[1]),
        pltpu.make_async_copy(s_hbm, field.at[1], load_sem.at[2]),
        pltpu.make_async_copy(d_hbm, d_in, load_sem.at[3]),
    ]
    loads[0].start()
    loads[1].start()

    def on_sub(by):
        return dom, lax.rem(sub + by + subs, subs)

    def on_dom(by):
        return lax.rem(dom + by + doms, doms), sub

    def on_level(by, to=sub):
        return height * depth + lax.rem(level + by + depth, depth), to

    def on_height(by):
        return lax.rem(height + by + heights, heights) * depth + level, sub

    def on_chip(by, to):
        return dom, lax.rem(chip + by, chips) * 2 + to

    near = [on_level(-1), on_level(1), on_height(-1), on_height(1)]
    greeted = [on_dom(-1), on_dom(1), on_sub(-1), on_sub(1)] + near
    barrier = pltpu.get_barrier_semaphore()
    for peer in greeted:
        pl.semaphore_signal(barrier, inc=1, device_id=peer, device_id_type=MESH)

    for load in loads[2:]:
        load.start()

    def pass_token(step):
        for peer in near:
            pl.semaphore_signal(token_sem.at[step], inc=1, device_id=peer, device_id_type=MESH)

    def x_message(k, f, way):
        return pltpu.make_async_remote_copy(
            src_ref=x_sent.at[k, f, way],
            dst_ref=x_got.at[k, f, way],
            send_sem=x_send.at[k, f, way],
            recv_sem=x_recv.at[k, f, way],
            device_id=on_sub(2 * way - 1),
            device_id_type=MESH,
        )

    def y_message(k, f, way, e):
        return pltpu.make_async_remote_copy(
            src_ref=y_sent.at[k, f, way, e],
            dst_ref=y_got.at[k, f, way, e],
            send_sem=y_send.at[k, f, way, e],
            recv_sem=y_recv.at[k, f, way, e],
            device_id=on_dom(2 * way - 1),
            device_id_type=MESH,
        )

    def through(lefts, e, rights, x):
        put_columns(rights.at[e], 0, x)
        return product(lefts[e], rights[e])

    def y_down(k, f, e, trace):
        y_sent[k, f, DOWN, e] = trace
        y_message(k, f, DOWN, e).start()

    def y_up(k, f, e):
        y_sent[k, f, UP, e] = product(left_y[e], right_y[e])
        y_message(k, f, UP, e).start()

    def x_down(k, f):
        x_sent[k, f, DOWN] = x_face(field.at[f], 0)
        x_message(k, f, DOWN).start()

    def x_up(k, f):
        trace = x_face(field.at[f], 3)
        for e in range(2):
            x_sent[k, f, UP, e] = through(left_up, e, right_up, trace[e])
        x_message(k, f, UP).start()

    for ref in (c_pad, right_up, right_in, left_y, right_y):
        ref[...] = jnp.zeros_like(ref)

    loads[0].wait()
    for e in range(2):
        for side, last in enumerate((sub == subs - 1, dom == doms - 1)):
            c_pad[e, side, 0:FACE, 0:FACE] = jnp.where(last, 0.0, c_in[e, side])
        c_pad[e, 2, 0:FACE, 0:FACE] = c_in[e, 2]
    for e in range(2):
        put_rows(left_y.at[e], 0, 0, FACE, c_pad[e, 1].T[:FACE])
        put_rows(left_up.at[e], 0, 0, FACE, c_pad[e, 0].T[:FACE])

    def first_traces(f):
        loads[1 + f].wait()
        for e in range(2):
            y_sent[0, f, DOWN, e] = y_low(field[f, e])
            put_columns(right_y.at[e], 0, y_high(field[f, e]))
            y_sent[0, f, UP, e] = product(left_y[e], right_y[e])
        x_sent[0, f, DOWN] = x_face(field.at[f], 0)
        trace = x_face(field.at[f], 3)
        for e in range(2):
            x_sent[0, f, UP, e] = through(left_up, e, right_up, trace[e])

    def first_sends(f):
        for e in range(2):
            for way in range(2):
                y_message(0, f, way, e).start()
        for way in range(2):
            x_message(0, f, way).start()

    first_traces(0)
    first_traces(1)
    pl.semaphore_wait(barrier, len(greeted))
    first_sends(0)
    first_sends(1)
    pass_token(0)

    for side in range(2):
        for e in range(2):
            put_rows(left_in.at[side, e], 0, 0, FACE, c_pad[e, side, 0:FACE])
    for e in range(2):
        put_columns(right_in.at[e], 0, c_pad[e, 1, 0:FACE])
        put_rows(left_y.at[e], 0, COLS, FACE, product(left_y[e, :, 0:COLS], right_in[e]))
    for ref in (z_pad, d_pad, left, right):
        ref[...] = jnp.zeros_like(ref)
    z_pad[0, pl.ds(3, FACE, stride=4), :] = c_pad[0, 2, 0:FACE]
    z_pad[1, pl.ds(0, FACE, stride=4), :] = -c_pad[0, 2].T[:FACE]
    loads[3].wait()
    for e in range(2):
        d_pad[e, 0:ROWS, 0:ROWS] = d_in[e]
        put_rows(left.at[0, e], 0, 0, ROWS, d_pad[e, 0:ROWS, :])
        put_rows(left.at[0, e], 0, 384, ROWS, z_pad[e])
        put_rows(left.at[1, e], 0, 384, ROWS, -z_pad[e])
        for i in range(3):
            rows = min(COLS, ROWS - i * COLS)
            for j in range(3):
                block = d_pad[e, j * COLS : (j + 1) * COLS, i * COLS : (i + 1) * COLS].T
                put_rows(left.at[1, e], i * COLS, j * COLS, ROWS, block[:rows])

    def local_part(f):
        flat = field.at[f].reshape(2, ROWS, COLS)
        for e in range(2):
            put_columns(right.at[e], 0, flat[e])
            put_columns(right.at[e], 384, flat[1 - e, pl.ds(3 * e, FACE, stride=4), :])
        for e in range(2):
            acc[f, e] = product(left[f, e], right[e]).reshape(5, 64, COLS)

    for f in range(2):
        local_part(f)
    sums[0, 0:1] = column_sums(field[1], field[0])

    for k in range(STEPS):
        more = k + 1 < STEPS
        for f in range(2):
            sign = 1.0 - 2.0 * f
            for way in (UP, DOWN):
                x_message(k, f, way).wait_recv()
            for e in range(2):
                into = through(left_in.at[0], e, right_in, x_got[k, f, DOWN, e]).reshape(5, 16, COLS)
                acc[f, e, :, 48:64] = acc[f, e, :, 48:64] + sign * into
                back = x_got[k, f, UP, e].reshape(5, 16, COLS)
                acc[f, e, :, 0:16] = acc[f, e, :, 0:16] - sign * back
            if more:
                for e in range(2):
                    put_columns(right_y.at[e], 0, y_high(acc[f, e]))

            def from_above(e):
                y_message(k, f, DOWN, e).wait_recv()
                put_columns(right_y.at[e], COLS, sign * y_got[k, f, DOWN, e])
                if more:
                    y_up(k + 1, f, e)

            def from_below(e):
                y_message(k, f, UP, e).wait_recv()
                if more:
                    y_down(k + 1, f, e, y_low(acc[f, e]) - sign * y_got[k, f, UP, e])

            def update(e):
                high = product(left_in[1, e], right_y[e, COLS:])
                field[f, e] = add_y(acc[f, e], -sign * y_got[k, f, UP, e], high)
                return column_sums(field[1, e], field[0, e])

            parts = []
            for e in range(2):
                from_below(e)
                from_above(e)
                parts.append(update(e))
            if more:
                x_down(k + 1, f)
                x_up(k + 1, f)
            elif f == 0:
                pltpu.make_async_copy(field.at[0], ob_hbm, store_sem.at[0]).start()
            moment = 2 * k + 1 + f
            sums[0, moment : moment + 1] = parts[0] + parts[1]
            step = 2 * k + f
            if step < TOKENS:
                pl.semaphore_wait(token_sem.at[step], len(near))
                if step + 1 < TOKENS:
                    pass_token(step + 1)
            if more and f == 1:
                local_part(0)
                local_part(1)

    def total_copy(stage, slot, peer, send=None):
        return pltpu.make_async_remote_copy(
            src_ref=sums.at[stage],
            dst_ref=sums_got.at[slot],
            send_sem=sums_send.at[slot if send is None else send],
            recv_sem=sums_recv.at[slot],
            device_id=peer,
            device_id_type=MESH,
        )

    def arrived(total, stage, first, count):
        for slot in range(first, first + count):
            total_copy(stage, slot, on_level(1)).wait_recv()
            total = total + sums_got[slot]
        return total

    inner, outer = on_chip(0, 0), on_chip(0, 1)
    across = far_first(chips)
    slot_in, slot_y = 2 * len(across), 2 * len(across) + 1
    slot_z = slot_y + heights - 1
    slot_out = slot_z + depth - 1

    def settle():
        pltpu.make_async_copy(field.at[1], os_hbm, store_sem.at[1]).start()
        for k in range(STEPS):
            for f in range(2):
                for way in range(2):
                    x_message(k, f, way).wait_send()
                    for e in range(2):
                        y_message(k, f, way, e).wait_send()
        for f in range(2):
            pltpu.make_async_copy(field.at[f], (ob_hbm, os_hbm)[f], store_sem.at[f]).wait()

    @pl.when(core == 0)
    def _():
        copies = [total_copy(0, i, on_chip(by, 1)) for i, by in enumerate(across)]
        copies.append(total_copy(0, slot_in, outer))
        for copy in copies:
            copy.start()
        settle()
        for copy in copies:
            copy.wait_send()
        total_copy(2, slot_out, outer).wait_recv()
        total_ref[...] = arrived(sums_got[slot_out], 2, slot_z, depth - 1)

    @pl.when(core == 1)
    def _():
        copies = [total_copy(0, len(across) + i, on_chip(by, 1)) for i, by in enumerate(across)]
        for copy in copies:
            copy.start()
        settle()
        for copy in copies:
            copy.wait_send()
        sums[1] = arrived(sums[0], 0, 0, slot_y)
        along_y = [total_copy(1, slot_y + i, on_height(by)) for i, by in enumerate(far_first(heights))]
        for copy in along_y:
            copy.start()
        for copy in along_y:
            copy.wait_send()
        sums[2] = arrived(sums[1], 1, slot_y, heights - 1)
        along_z = []
        for i in range(depth - 1):
            after = (i + depth - level) // depth
            place = height * depth + i + after
            slot = slot_z + level - 1 + after
            along_z.append(total_copy(2, slot, (place, chip * 2), slot_z + i))
            along_z.append(total_copy(2, slot, (place, sub), slot_out + 1 + i))
        along_z.append(total_copy(2, slot_out, inner))
        for copy in along_z:
            copy.start()
        for copy in along_z:
            copy.wait_send()
        total_ref[...] = arrived(sums[2], 2, slot_z, depth - 1)


def pin(x):
    return pltpu.with_memory_space_constraint(x, pltpu.HBM)


def finish(scale, b_hbm, s_hbm, total_ref, ob_hbm, os_hbm, moments_hbm, moments_ref, moments_sem, sem):
    copies = [
        pltpu.make_async_copy(b_hbm.at[e], ob_hbm.at[e], sem.at[0, e]) for e in range(2)
    ] + [pltpu.make_async_copy(s_hbm.at[e], os_hbm.at[e], sem.at[1, e]) for e in range(2)]
    for copy in copies:
        copy.start()
    total = total_ref[...] * scale
    for i in range(STEPS + 1):
        moments_ref[i] = total[i : i + STEPS + 1]
    copies.append(pltpu.make_async_copy(moments_ref, moments_hbm, moments_sem))
    copies[-1].start()
    for copy in copies:
        copy.wait()


def solution(mesh):
    doms, subs = mesh.shape["dom"], mesh.shape["sub"]
    depth = 12
    slots = 2 * (subs // 2 - 1) + 1 + (doms // depth - 1) + (depth - 1) + 1
    anywhere = pl.BlockSpec(memory_space=pl.ANY)
    inside = pl.BlockSpec(memory_space=pltpu.VMEM)
    grant = 40 * 1024 * 1024

    def body(diagonal, coupling, start_block, shadow_block):
        count = 2 * ROWS * doms * subs
        field_shape = jax.ShapeDtypeStruct((2, 5, 64, COLS), F32)
        moments_shape = jax.ShapeDtypeStruct((STEPS + 1, STEPS + 1, COLS), F32)
        total_shape = jax.ShapeDtypeStruct((SUMS, COLS), F32)
        powers = pl.pallas_call(
            functools.partial(kernel, (doms, subs, depth)),
            out_shape=(field_shape, field_shape, total_shape),
            in_specs=[anywhere] * 4,
            out_specs=(anywhere, anywhere, inside),
            scratch_shapes=[
                pltpu.VMEM((2, ROWS, ROWS), F32),
                pltpu.VMEM((2, 3, FACE, FACE), F32),
                pltpu.VMEM((2, 2, 5, 64, COLS), F32),
                pltpu.VMEM((2, 2, 5, 64, COLS), F32),
                pltpu.VMEM((2, 384, 384), F32),
                pltpu.VMEM((2, 3, COLS, COLS), F32),
                pltpu.VMEM((2, ROWS, COLS), F32),
                pltpu.VMEM((2, 2, 2 * ROWS, 512), BF16),
                pltpu.VMEM((2, 2 * FACE, COLS), BF16),
                pltpu.VMEM((2, 2, 2 * FACE, COLS), BF16),
                pltpu.VMEM((2, 2 * FACE, 256), BF16),
                pltpu.VMEM((2, 512, 256), BF16),
                pltpu.VMEM((2, COLS, 256), BF16),
                pltpu.VMEM((2, COLS, 256), BF16),
                pltpu.VMEM((2, 256, 256), BF16),
                *[pltpu.VMEM((STEPS, 2, 2, 2, FACE, COLS), F32)] * 4,
                pltpu.VMEM((3, SUMS, COLS), F32),
                pltpu.VMEM((slots, SUMS, COLS), F32),
                pltpu.SemaphoreType.DMA((4,)),
                pltpu.SemaphoreType.DMA((2,)),
                pltpu.SemaphoreType.DMA((STEPS, 2, 2)),
                pltpu.SemaphoreType.DMA((STEPS, 2, 2)),
                pltpu.SemaphoreType.DMA((STEPS, 2, 2, 2)),
                pltpu.SemaphoreType.DMA((STEPS, 2, 2, 2)),
                pltpu.SemaphoreType.DMA((slots + depth - 1,)),
                pltpu.SemaphoreType.DMA((slots,)),
                pltpu.SemaphoreType.REGULAR((TOKENS,)),
            ],
            compiler_params=pltpu.CompilerParams(
                collective_id=0, has_side_effects=True, vmem_limit_bytes=grant
            ),
            name="powers",
        )(
            pin(diagonal.reshape(2, ROWS, ROWS)),
            pin(coupling.reshape(2, 3, FACE, FACE)),
            pin(start_block.reshape(2, 5, 64, COLS)),
            pin(shadow_block.reshape(2, 5, 64, COLS)),
        )
        basis, shadow, moments = pl.pallas_call(
            functools.partial(finish, 1.0 / count),
            out_shape=(field_shape, field_shape, moments_shape),
            in_specs=[anywhere, anywhere, inside],
            out_specs=(anywhere, anywhere, anywhere),
            scratch_shapes=[pltpu.VMEM((STEPS + 1, STEPS + 1, COLS), F32), pltpu.SemaphoreType.DMA, pltpu.SemaphoreType.DMA((2, 2))],
            compiler_params=pltpu.CompilerParams(vmem_limit_bytes=grant),
            name="finish",
        )(*powers)
        return basis.reshape(start_block.shape), shadow.reshape(start_block.shape), moments

    placed = P("sub", "dom", None, None, None)
    return jax.shard_map(
        body,
        mesh=mesh,
        in_specs=(placed, P("sub", "dom", None, None, None, None), placed, placed),
        out_specs=(placed, placed, P()),
        check_vma=False,
    )
```
